32 devices in a mesh: dp: 4 (over y, x), vocab: 8 (over z, core).
Axes of the slice: x: 2, y: 2, z: 4, core: 2. Of those that a mesh axis runs over, the one named last changes fastest.
Arguments:
- hidden: bfloat16 [128, 3584], P(('dp', 'vocab')), may hold values from -6 to 6
- head_weight: bfloat16 [3584, 256000], P(None, ('dp', 'vocab')), may hold values from -0.75 to 0.75
- teacher_ids: int32 [128, 128], P(('dp', 'vocab')), may hold values from 0 to 255999
- teacher_probs: float32 [128, 128], P(('dp', 'vocab')), may hold values from 0.0001 to 0.015
- target_ids: int32 [128], P(('dp', 'vocab')), may hold values from 0 to 255999
Outputs:
- token_loss: float32 [128], P(('dp', 'vocab'))
- hidden_grad: bfloat16 [128, 3584], P(('dp', 'vocab'))
The draws below stay inside these ranges and needn't reach their ends.
All inputs are finite; a program needn't handle non-finite values.
Results may differ from the reference program's by a relative error of at most 0.004.
Values may be sent and summed in bfloat16 or wider, within the bound.
A program may use at most 128 MiB of HBM per device.

```python
import math
import jax
import jax.numpy as jnp
import numpy as np
from jax import lax

D = 3584
V = 256000
K = 128
TOKENS = 128


def plant(result, rng, least, top_value):
    longest = result.shape.index(max(result.shape))
    spots = []
    for shift in (0, 1):
        where = [jax.random.randint(jax.random.fold_in(rng, axis), (), 0, length) for axis, length in enumerate(result.shape)]
        where[longest] = (where[longest] + shift) % result.shape[longest]
        spots.append(tuple(where))
    return result.at[spots[0]].set(least).at[spots[1]].set(top_value)


def block_scale(rng, shape, shards, smallest, largest):
    level, own = 1.0, jax.random.fold_in(rng, 6)
    for position, parts in shards:
        draws = jnp.exp(jax.random.uniform(jax.random.fold_in(own, position), (parts,), jnp.float32, smallest / len(shards), largest / len(shards)))
        level = level * jnp.repeat(draws, shape[position] // parts).reshape([-1 if axis == position else 1 for axis in range(len(shape))])
    return level


def wide_ids(rng, extent, count, skew):
    weights = [min(1 << octave, count + 1 - (1 << octave)) * (1 << 20) // math.isqrt((1 << octave) ** skew) + 1 for octave in range((count + 1).bit_length()) if 1 << octave <= count]
    deviation = 1 + sum(weights) // (1 << 30)
    listing = np.cumsum(np.array([max(1, weight // deviation) for weight in weights]))
    pick = jax.random.randint(jax.random.fold_in(rng, 1), extent, 0, int(listing[len(weights) - 1]))
    start = jnp.left_shift(1, jnp.searchsorted(jnp.asarray(listing, jnp.int32), pick, side="right").astype(jnp.int32))
    grade = start - 1 + jax.random.randint(jax.random.fold_in(rng, 4), extent, 0, 1 << 30) % jnp.minimum(start, count + 1 - start)
    return jax.random.permutation(jax.random.fold_in(rng, 2), count)[grade].astype(jnp.int32)


def bell_draw(rng, shape, deviation, reach, shards=(), held_as=jnp.bfloat16):
    entries = deviation * jax.random.normal(rng, shape, jnp.float32)
    if shards:
        entries = entries * block_scale(rng, shape, shards, -0.22, 0.18)
    return jnp.clip(entries, -reach, reach).astype(held_as)


def setup_inputs(seed: int = 0) -> dict:
    keys = jax.random.split(jax.random.key(seed), 6)
    return {
        "hidden": bell_draw(keys[0], (TOKENS, D), 1.0, 6.0, ((0, 32),)),
        "head_weight": bell_draw(keys[1], (D, V), 64 ** -0.5, 0.75, ((1, 32),)),
        "teacher_ids": plant(wide_ids(keys[2], (TOKENS, K), V, 2), jax.random.fold_in(keys[2], 3), 0, V - 1).astype(jnp.int32),
        "teacher_probs": jnp.clip(jnp.exp(math.log(0.015) - 5.0106353 * jax.random.uniform(keys[3], (TOKENS, K), jnp.float32) ** block_scale(keys[3], (TOKENS, K), ((0, 32),), -0.2, 0.2)), 0.0001, 0.015),
        "target_ids": plant(jax.random.randint(keys[4], (TOKENS,), 0, V), jax.random.fold_in(keys[4], 1), 0, V - 1).astype(jnp.int32),
    }


SOFT_CAP = 30.0
CE_WEIGHT = 0.5
LOSS_SCALE = 8.0


def teacher_terms(capped, first_column, teacher_ids, teacher_probs, target_ids):
    slice_width = capped.shape[1]
    inside = (teacher_ids >= first_column) & (teacher_ids < first_column + slice_width)
    local_column = jnp.clip(teacher_ids - first_column, 0, slice_width - 1).astype(jnp.int32)
    picked = jnp.take_along_axis(capped, local_column, axis=1)
    teacher_dot = jnp.sum(jnp.where(inside, teacher_probs * picked, 0.0), axis=1)
    columns = first_column + jnp.arange(slice_width, dtype=jnp.int32)
    target_hit = columns[None, :] == target_ids[:, None]
    target_logit = jnp.sum(jnp.where(target_hit, capped, 0.0), axis=1)
    return inside, local_column, target_hit, teacher_dot, target_logit


def logit_grads(capped, log_total, teacher_sum, inside, local_column, teacher_probs, target_hit):
    token_count = capped.shape[0]
    row_index = jnp.broadcast_to(jnp.arange(token_count, dtype=jnp.int32)[:, None], local_column.shape)
    sparse = jnp.zeros(capped.shape, jnp.float32).at[row_index, local_column].add(jnp.where(inside, teacher_probs, 0.0))
    softmax_rows = jnp.exp(capped - log_total[:, None])
    onehot = jnp.where(target_hit, 1.0, 0.0)
    raw_grads = LOSS_SCALE * ((teacher_sum + CE_WEIGHT)[:, None] * softmax_rows - sparse - CE_WEIGHT * onehot)
    return (raw_grads * (1.0 - (capped / SOFT_CAP) ** 2)).astype(jnp.bfloat16)


def reference(hidden, head_weight, teacher_ids, teacher_probs, target_ids):
    blocks = 32
    slice_width = V // blocks
    token_count = hidden.shape[0]

    def capped_block(block_index):
        first_column = (block_index * slice_width).astype(jnp.int32)
        block = lax.dynamic_slice_in_dim(head_weight, first_column, slice_width, 1)
        raw_logits = jnp.dot(hidden, block, preferred_element_type=jnp.float32)
        return first_column, block, SOFT_CAP * jnp.tanh(raw_logits / SOFT_CAP)

    def block_stats(totals, block_index):
        first_column, block, capped = capped_block(block_index)
        terms = teacher_terms(capped, first_column, teacher_ids, teacher_probs, target_ids)
        exp_total = jnp.sum(jnp.exp(capped), axis=1)
        return (totals[0] + exp_total, totals[1] + terms[3], totals[2] + terms[4]), None

    zeros_rows = jnp.zeros((token_count,), jnp.float32)
    indices = jnp.arange(blocks, dtype=jnp.int32)
    (exp_sum, teacher_dot, target_logit), _ = lax.scan(block_stats, (zeros_rows, zeros_rows, zeros_rows), indices)
    log_total = jnp.log(exp_sum)
    teacher_sum = jnp.sum(teacher_probs, axis=1)
    token_loss = jnp.sum(teacher_probs * jnp.log(teacher_probs), axis=1) - teacher_dot + teacher_sum * log_total + CE_WEIGHT * (log_total - target_logit)

    def block_grads(accum, block_index):
        first_column, block, capped = capped_block(block_index)
        inside, local_column, target_hit, _, _ = teacher_terms(capped, first_column, teacher_ids, teacher_probs, target_ids)
        grads = logit_grads(capped, log_total, teacher_sum, inside, local_column, teacher_probs, target_hit)
        return accum + jnp.einsum("tv,dv->td", grads, block, preferred_element_type=jnp.float32), None

    accum, _ = lax.scan(block_grads, jnp.zeros((token_count, D), jnp.float32), indices)
    return token_loss, accum.astype(jnp.bfloat16)
```

```python
import functools
import jax
import jax.numpy as jnp
from jax import lax
from jax.experimental import pallas as pl
from jax.experimental.pallas import tpu as pltpu
from jax.sharding import PartitionSpec as P

SOFT_CAP = 30.0
CE_WEIGHT = 0.5
LOSS_SCALE = 8.0
BLOCK = 640
CHUNK = 512
LANES = 128
PACK = 16
AXES = ("dp", "vocab")
MESH = pl.DeviceIdType.MESH
NT = (((1,), (1,)), ((), ()))


def remote(src, dst, send, recv, peer):
    return pltpu.make_async_remote_copy(
        src_ref=src, dst_ref=dst, send_sem=send, recv_sem=recv,
        device_id=peer, device_id_type=MESH)


def fused_kernel(nd, nv, hid_in, ids_in, probs_in, targets_in, w_hbm, loss_ref, grad_ref,
                 w_ref, hid, near, near32, small, cells, grads, probs, exp_part, dot_part,
                 column, totals, slots_v, slots_d, own1, send1, send2, own2, send3, recv3,
                 w_sem, zs_send, zs_recv, zh_send, zh_recv, ds_send, ds_recv, dh_send, dh_recv,
                 cs_send, cs_recv, ch_send, ch_recv, tv_send, tv_recv, td_send, td_recv,
                 r1_send, r1_recv, r2_send, r2_recv, r3_send, r3_recv):
    local_tokens, depth = hid_in.shape
    tokens = hid.shape[0]
    width = w_ref.shape[0]
    kept = ids_in.shape[1]
    nz = nv // 2
    rows = nz * local_tokens
    half = nd * rows
    chunks = depth // CHUNK
    d, v = lax.axis_index("dp"), lax.axis_index("vocab")
    z, k = v // 2, lax.rem(v, 2)
    mine = d * 2 + k
    zs = [lax.rem(z + o, nz) for o in range(1, nz)]
    dps = [lax.rem(d + o, nd) for o in range(1, nd)]
    sibling = (d, z * 2 + 1 - k)
    z_peer = lambda q: (d, q * 2 + k)
    d_peer = lambda q: (q, v)

    full_blocks, tail = width // BLOCK, width % BLOCK
    pieces = full_blocks + (tail > 0)

    def w_copy(j, size):
        at = pl.ds(pl.multiple_of(j * BLOCK, BLOCK), size)
        return pltpu.make_async_copy(w_hbm.at[at], w_ref.at[at], w_sem.at[j])

    def start_w(j, carry):
        w_copy(j, BLOCK).start()
        return carry

    lax.fori_loop(0, full_blocks, start_w, 0)
    if tail:
        w_copy(full_blocks, tail).start()

    own_block = mine * nz + z
    for i in range(local_tokens):
        small[own_block, 2 * local_tokens + i:2 * local_tokens + i + 1, :] = jnp.full(
            (1, kept), targets_in[i], jnp.int32).astype(jnp.float32)
    small[own_block, 0:local_tokens, :] = ids_in[...].astype(jnp.float32)
    small[own_block, local_tokens:2 * local_tokens, :] = probs_in[...]
    near[z] = hid_in[...]

    barrier = pltpu.get_barrier_semaphore()
    peers_v = [(d, lax.rem(v + o, nv)) for o in range(1, nv)]
    peers_d = [d_peer(q) for q in dps]
    for peer in peers_v + peers_d:
        pl.semaphore_signal(barrier, inc=1, device_id=peer, device_id_type=MESH)
    pl.semaphore_wait(barrier, nv + nd - 2)

    sent = []

    def go(copy):
        copy.start()
        sent.append(copy)

    for o, q in enumerate(zs):
        go(remote(small.at[own_block], small.at[own_block], zs_send.at[o], zs_recv.at[z],
                  z_peer(q)))
    for o, q in enumerate(zs):
        go(remote(hid_in, near.at[z], zh_send.at[o], zh_recv.at[z], z_peer(q)))
    for o, q in enumerate(zs):
        at = small.at[mine * nz + q]
        remote(at, at, zs_send.at[o], zs_recv.at[q], z_peer(q)).wait_recv()

    def small_at(group):
        return small.at[pl.ds(group * nz, nz)]

    def hid_at(group):
        return hid.at[pl.ds(pl.multiple_of(group * rows, rows), rows)]

    at = small_at(mine)
    for o, q in enumerate(dps):
        go(remote(at, at, ds_send.at[o], ds_recv.at[d], d_peer(q)))
    go(remote(at, at, cs_send.at[d], cs_recv.at[d], sibling))

    for o, q in enumerate(zs):
        remote(hid_in, near.at[q], zh_send.at[o], zh_recv.at[q], z_peer(q)).wait_recv()
    for q in range(nz):
        near32[q * local_tokens:(q + 1) * local_tokens, :] = near[q].astype(jnp.float32)
    hid[pl.ds(pl.multiple_of(mine * rows, rows), rows), :] = near32[...].astype(jnp.bfloat16)
    at = hid_at(mine)
    for o, q in enumerate(dps):
        go(remote(at, at, dh_send.at[o], dh_recv.at[d], d_peer(q)))
    go(remote(at, at, ch_send.at[d], ch_recv.at[d], sibling))

    for o, q in enumerate(dps):
        at = small_at(q * 2 + k)
        remote(at, at, ds_send.at[o], ds_recv.at[q], d_peer(q)).wait_recv()
        go(remote(at, at, cs_send.at[q], cs_recv.at[q], sibling))
    for q in range(nd):
        at = small_at(q * 2 + 1 - k)
        remote(at, at, cs_send.at[q], cs_recv.at[q], sibling).wait_recv()

    groups = pl.cdiv(width, LANES)
    group_rows = 16 * pl.cdiv(groups, 16)
    offset = (d * nv + v) * width
    group_row = lax.broadcasted_iota(jnp.int32, (group_rows, kept), 0)
    lane_row = lax.broadcasted_iota(jnp.int32, (LANES, kept), 0)
    flat = group_row * LANES + lax.broadcasted_iota(jnp.int32, (group_rows, LANES), 1)
    per_step = 8 // local_tokens

    def scatter(step, carry):
        first = pl.multiple_of(step * 8, 8)
        found = []
        for i in range(8):
            block = step * per_step + i // local_tokens
            r = i % local_tokens
            ids = small[block, r:r + 1, :].astype(jnp.int32) - offset
            p = small[block, local_tokens + r:local_tokens + r + 1, :]
            target = small[block, 2 * local_tokens + r:2 * local_tokens + r + 1, :]
            target = target.astype(jnp.int32) - offset
            probs[pl.ds(first + i, 1), :] = p
            high = p.astype(jnp.bfloat16).astype(jnp.float32)
            inside = group_row == (ids >> 7)
            left = jnp.concatenate(
                [jnp.where(inside, high, 0.0), jnp.where(inside, p - high, 0.0)],
                axis=0).astype(jnp.bfloat16)
            right = jnp.where(lane_row == (ids & 127), 1.0, 0.0).astype(jnp.bfloat16)
            both = lax.dot_general(left, right, NT, preferred_element_type=jnp.float32)
            found.append(both[:group_rows] + both[group_rows:]
                         + jnp.where(flat == target, CE_WEIGHT, 0.0))
        cells[:, pl.ds(first, 8), :] = jnp.swapaxes(jnp.stack(found, axis=0), 0, 1)[:groups]
        return carry

    lax.fori_loop(0, tokens // 16, scatter, 0)
    for o, q in enumerate(dps):
        at = hid_at(q * 2 + k)
        remote(at, at, dh_send.at[o], dh_recv.at[q], d_peer(q)).wait_recv()
        go(remote(at, at, ch_send.at[q], ch_recv.at[q], sibling))
    lax.fori_loop(tokens // 16, tokens // 8, scatter, 0)
    for q in range(nd):
        at = hid_at(q * 2 + 1 - k)
        remote(at, at, ch_send.at[q], ch_recv.at[q], sibling).wait_recv()
    for copy in sent:
        copy.wait_send()
    sent.clear()

    exp_part[...] = jnp.zeros_like(exp_part)
    dot_part[...] = jnp.zeros_like(dot_part)

    def block(j, size):
        w_copy(j, size).wait()
        w = w_ref[pl.ds(pl.multiple_of(j * BLOCK, BLOCK), size), :]
        logits = lax.dot_general(w, hid[...], NT, preferred_element_type=jnp.float32).T
        for i in range(pl.cdiv(size, LANES)):
            n = min(LANES, size - i * LANES)
            group = j * (BLOCK // LANES) + i
            ratio = jnp.tanh(logits[:, i * LANES:i * LANES + n] * (1.0 / SOFT_CAP))
            capped = SOFT_CAP * ratio
            slope = 1.0 - ratio * ratio
            exps = jnp.exp(capped)
            sparse = cells[group, :, 0:n]
            cells[group, :, 0:n] = exps * slope
            grads[:, pl.ds(pl.multiple_of(group * LANES, LANES), n)] = (
                sparse * slope).astype(jnp.bfloat16)
            exp_part[:, 0:n] += exps
            dot_part[:, 0:n] += capped * sparse

    def full_block(j, carry):
        block(j, BLOCK)
        return carry

    lax.fori_loop(0, full_blocks, full_block, 0)
    if tail:
        block(full_blocks, tail)

    totals[...] = jnp.zeros_like(totals)
    totals[0:1, :] = jnp.sum(exp_part[...].T, axis=0, keepdims=True)
    totals[1:2, :] = jnp.sum(dot_part[...].T, axis=0, keepdims=True)
    for peers, me, slots, send, recv, axis in (
        (peers_v, v, slots_v, tv_send, tv_recv, 1),
        (peers_d, d, slots_d, td_send, td_recv, 0),
    ):
        slots[me] = totals[...]
        for o, peer in enumerate(peers):
            go(remote(slots.at[me], slots.at[me], send.at[o], recv.at[me], peer))
        for o, peer in enumerate(peers):
            at = slots.at[peer[axis]]
            remote(at, at, send.at[o], recv.at[peer[axis]], peer).wait_recv()
        totals[...] = jnp.sum(slots[...], axis=0)
    for copy in sent:
        copy.wait_send()
    sent.clear()

    spread = lambda row: jnp.broadcast_to(row, (LANES, tokens)).T
    exp_sum = spread(totals[0:1, :])
    exp_part[...] = exp_sum
    dot_part[...] = spread(totals[1:2, :])
    teacher_sum = jnp.sum(probs[...], axis=1, keepdims=True)
    column[...] = LOSS_SCALE * (teacher_sum + CE_WEIGHT) / exp_sum

    own_row = mine * rows + z * local_tokens
    for i in range(local_tokens):
        p = probs_in[i:i + 1, :]
        loss_ref[i:i + 1, :] = (
            jnp.sum(p * jnp.log(p), axis=1, keepdims=True)
            - dot_part[pl.ds(own_row + i, 1), :]
            + (jnp.sum(p, axis=1, keepdims=True) + CE_WEIGHT)
            * jnp.log(exp_part[pl.ds(own_row + i, 1), :]))

    def scale_group(group, n):
        at = pl.ds(pl.multiple_of(group * LANES, LANES), n)
        grads[:, at] = (column[:, 0:n] * cells[group, :, 0:n]
                        - LOSS_SCALE * grads[:, at].astype(jnp.float32)).astype(jnp.bfloat16)

    def scale_full(group, carry):
        scale_group(group, LANES)
        return carry

    lax.fori_loop(0, width // LANES, scale_full, 0)
    if width % LANES:
        scale_group(width // LANES, width % LANES)

    def cols(c):
        return pl.ds(pl.multiple_of(c * CHUNK, CHUNK), CHUNK)

    def copy1(c):
        return remote(send1.at[lax.rem(c, 2)], hid.at[pl.ds(0, half), cols(c)],
                      r1_send.at[c], r1_recv.at[c], sibling)

    def copy2(c, o, q, source):
        return remote(send2.at[lax.rem(c, 2), pl.ds(pl.multiple_of(q * rows, rows), rows)],
                      hid.at[pl.ds(pl.multiple_of(half + source * rows, rows), rows), cols(c)],
                      r2_send.at[c, o], r2_recv.at[c, source], d_peer(q))

    def copy3(c, o, q, source):
        return remote(send3.at[lax.rem(c, 2), q], recv3.at[c, source],
                      r3_send.at[c, o], r3_recv.at[c, source], z_peer(q))

    def grad_step(c, carry):
        @pl.when(c < chunks)
        def _():
            acc = jnp.dot(grads[...], w_ref[:, cols(c)], preferred_element_type=jnp.float32)
            acc = acc.reshape(nd, 2, rows, CHUNK)
            slot = lax.rem(c, 2)
            own1[slot] = jnp.where(k == 0, acc[:, 0], acc[:, 1]).reshape(half, CHUNK)
            send1[slot] = jnp.where(k == 0, acc[:, 1], acc[:, 0]).reshape(half, CHUNK).astype(
                jnp.bfloat16)
            copy1(c).start()

        @pl.when((c >= 1) & (c < chunks + 1))
        def _():
            b = c - 1
            slot = lax.rem(b, 2)
            copy1(b).wait()
            total = own1[slot] + hid[0:half, cols(b)].astype(jnp.float32)
            own1[slot] = total
            send2[slot] = total.astype(jnp.bfloat16)
            for o, q in enumerate(dps):
                copy2(b, o, q, d).start()
            own2[slot] = own1[slot, pl.ds(pl.multiple_of(d * rows, rows), rows), :]

        @pl.when((c >= 2) & (c < chunks + 2))
        def _():
            b = c - 2
            slot = lax.rem(b, 2)
            total = own2[slot]
            for o, q in enumerate(dps):
                copy2(b, o, q, q).wait_recv()
                at = pl.ds(pl.multiple_of(half + q * rows, rows), rows)
                total = total + hid[at, cols(b)].astype(jnp.float32)
            for o, q in enumerate(dps):
                copy2(b, o, q, d).wait_send()
            for q in range(nz):
                send3[slot, q] = total[q * local_tokens:(q + 1) * local_tokens]
            for o, q in enumerate(zs):
                copy3(b, o, q, z).start()
            recv3[b, z] = send3[slot, z]

        @pl.when(c >= 3)
        def _():
            b = c - 3
            for o, q in enumerate(zs):
                copy3(b, o, q, q).wait_recv()
            for o, q in enumerate(zs):
                copy3(b, o, q, z).wait_send()
            total = recv3[b, 0]
            for q in range(1, nz):
                total = total + recv3[b, q]
            grad_ref[:, cols(b)] = total.astype(jnp.bfloat16)

        return carry

    lax.fori_loop(0, chunks + 3, grad_step, 0)


def per_device(nd, nv, hidden, head_weight, teacher_ids, teacher_probs, target_ids):
    local_tokens, depth = hidden.shape
    width = head_weight.shape[1]
    kept = teacher_ids.shape[1]
    count = nd * nv
    tokens = count * local_tokens
    nz = nv // 2
    rows = nz * local_tokens
    half = nd * rows
    chunks = depth // CHUNK
    groups = pl.cdiv(width, LANES)
    f32, bf16 = jnp.float32, jnp.bfloat16
    sems = lambda *shape: pltpu.SemaphoreType.DMA(shape)
    vmem = pl.BlockSpec(memory_space=pltpu.VMEM)
    loss, grad = pl.pallas_call(
        functools.partial(fused_kernel, nd, nv),
        in_specs=[vmem, vmem, vmem, pl.BlockSpec(memory_space=pltpu.SMEM),
                  pl.BlockSpec(memory_space=pl.ANY)],
        out_specs=[vmem, vmem],
        out_shape=[jax.ShapeDtypeStruct((local_tokens, LANES), f32),
                   jax.ShapeDtypeStruct((local_tokens, depth), bf16)],
        scratch_shapes=[
            pltpu.VMEM((width, depth), bf16),
            pltpu.VMEM((tokens, depth), bf16),
            pltpu.VMEM((nz, local_tokens, depth), bf16),
            pltpu.VMEM((rows, depth), f32),
            pltpu.VMEM((count, PACK, kept), f32),
            pltpu.VMEM((groups, tokens, LANES), f32),
            pltpu.VMEM((tokens, width), bf16),
            pltpu.VMEM((tokens, kept), f32),
            pltpu.VMEM((tokens, LANES), f32),
            pltpu.VMEM((tokens, LANES), f32),
            pltpu.VMEM((tokens, LANES), f32),
            pltpu.VMEM((8, tokens), f32),
            pltpu.VMEM((nv, 8, tokens), f32),
            pltpu.VMEM((nd, 8, tokens), f32),
            pltpu.VMEM((2, half, CHUNK), f32),
            pltpu.VMEM((2, half, CHUNK), bf16),
            pltpu.VMEM((2, half, CHUNK), bf16),
            pltpu.VMEM((2, rows, CHUNK), f32),
            pltpu.VMEM((2, nz, local_tokens, CHUNK), f32),
            pltpu.VMEM((chunks, nz, local_tokens, CHUNK), f32),
            sems(pl.cdiv(width, BLOCK)),
            sems(nz), sems(nz), sems(nz), sems(nz),
            sems(nd), sems(nd), sems(nd), sems(nd),
            sems(nd), sems(nd), sems(nd), sems(nd),
            sems(nv), sems(nv), sems(nd), sems(nd),
            sems(chunks), sems(chunks),
            sems(chunks, nd), sems(chunks, nd),
            sems(chunks, nz), sems(chunks, nz),
        ],
        compiler_params=pltpu.CompilerParams(
            collective_id=0, has_side_effects=True, vmem_limit_bytes=64 * 1024 * 1024),
        cost_estimate=pl.CostEstimate(
            flops=4 * tokens * depth * width, bytes_accessed=2 * depth * width,
            transcendentals=2 * tokens * width),
        name="fused_head",
    )(hidden, teacher_ids, teacher_probs, target_ids, head_weight.T)
    return loss[:, 0], grad


def solution(mesh):
    in_specs = (
        P(AXES, None),
        P(None, AXES),
        P(AXES, None),
        P(AXES, None),
        P(AXES),
    )
    out_specs = (P(AXES), P(AXES, None))
    return jax.shard_map(
        functools.partial(per_device, mesh.shape["dp"], mesh.shape["vocab"]),
        mesh=mesh, in_specs=in_specs, out_specs=out_specs, check_vma=False
    )
```

```python
import functools
import jax
import jax.numpy as jnp
from jax import lax
from jax.experimental import pallas as pl
from jax.experimental.pallas import tpu as pltpu
from jax.sharding import PartitionSpec as P

SOFT_CAP = 30.0
CE_WEIGHT = 0.5
LOSS_SCALE = 8.0
BLOCK = 640
CHUNK = 768
LANES = 128
PIECES = 2
LAG = 2
AXES = ("dp", "vocab")
MESH = pl.DeviceIdType.MESH
NT = (((1,), (1,)), ((), ()))


def remote(src, dst, send, recv, peer):
    return pltpu.make_async_remote_copy(
        src_ref=src, dst_ref=dst, send_sem=send, recv_sem=recv,
        device_id=peer, device_id_type=MESH)


def fused_kernel(nd, nv, hid_hbm, ids_hbm, probs_hbm, targets_hbm, w_hbm, out_hbm,
                 ids_in, probs_in, targets_in, out_ref, in_sem, out_sem, w_ref, hid, near, small, cells, grads, probs, exp_part, dot_part,
                 column, totals, slots_v, slots_d, recv3,
                 w_sem, zs_send, zs_recv, zh_send, zh_recv, ds_send, ds_recv, dh_send, dh_recv,
                 cs_send, cs_recv, ch_send, ch_recv, tv_send, tv_recv, td_send, td_recv,
                 r1_send, r1_recv, r2_send, r2_recv, r3_send, r3_recv):
    local_tokens, depth = hid_hbm.shape
    tokens = hid.shape[0]
    width = w_ref.shape[0]
    kept = ids_in.shape[1]
    nz = nv // 2
    rows = nz * local_tokens
    half = nd * rows
    starts = range(0, depth, CHUNK)
    chunks = len(starts)
    d, v = lax.axis_index("dp"), lax.axis_index("vocab")
    z, k = v // 2, lax.rem(v, 2)
    mine = d * 2 + k
    zs = [lax.rem(z + o, nz) for o in range(1, nz)]
    dps = [lax.rem(d + o, nd) for o in range(1, nd)]
    sibling = (d, z * 2 + 1 - k)
    z_peer = lambda q: (d, q * 2 + k)
    d_peer = lambda q: (q, v)

    full_blocks, tail = width // BLOCK, width % BLOCK
    pieces = full_blocks + (tail > 0)

    inputs = [
        pltpu.make_async_copy(src, dst, in_sem.at[i])
        for i, (src, dst) in enumerate((
            (ids_hbm, ids_in), (probs_hbm, probs_in), (targets_hbm, targets_in),
            (hid_hbm, near.at[z])))
    ]
    for copy in inputs:
        copy.start()

    barrier = pltpu.get_barrier_semaphore()
    peers_v = [(d, lax.rem(v + o, nv)) for o in range(1, nv)]
    peers_d = [d_peer(q) for q in dps]
    for peer in peers_v + peers_d:
        pl.semaphore_signal(barrier, inc=1, device_id=peer, device_id_type=MESH)

    def w_copy(j, size):
        at = pl.ds(pl.multiple_of(j * BLOCK, BLOCK), size)
        return pltpu.make_async_copy(w_hbm.at[at], w_ref.at[at], w_sem.at[j])

    def start_w(j, carry):
        w_copy(j, BLOCK).start()
        return carry

    lax.fori_loop(0, full_blocks, start_w, 0)
    if tail:
        w_copy(full_blocks, tail).start()

    for copy in inputs:
        copy.wait()
    own_block = mine * nz + z
    lane = lax.broadcasted_iota(jnp.int32, (1, kept), 1)
    target_row = jnp.zeros((1, kept), jnp.int32)
    for i in range(local_tokens):
        target_row = jnp.where(lane == i, targets_in[i], target_row)
    small[own_block, 0:local_tokens, :] = ids_in[...].astype(jnp.float32)
    small[own_block, local_tokens:2 * local_tokens, :] = probs_in[...]
    small[own_block, 2 * local_tokens:, :] = target_row.astype(jnp.float32)

    pl.semaphore_wait(barrier, nv + nd - 2)

    sent = []
    part = depth // PIECES

    def go(copy):
        copy.start()
        sent.append(copy)

    def small_at(group):
        return small.at[pl.ds(group * nz, nz)]

    def hid_at(group, p):
        return hid.at[pl.ds(pl.multiple_of(group * rows, rows), rows), pl.ds(p * part, part)]

    def near_copy(o, q, source, p):
        at = pl.ds(p * part, part)
        return remote(near.at[source, :, at], near.at[source, :, at],
                      zh_send.at[p, o], zh_recv.at[p, source], z_peer(q))

    def to_sibling(source, p):
        at = hid_at(source * 2 + k, p)
        go(remote(at, at, ch_send.at[p, source], ch_recv.at[p, source], sibling))

    def to_dp(o, q, p):
        at = hid_at(mine, p)
        go(remote(at, at, dh_send.at[p, o], dh_recv.at[p, d], d_peer(q)))

    def from_dp(source, p):
        at = hid_at(source * 2 + k, p)
        remote(at, at, dh_send.at[p, 0], dh_recv.at[p, source], d_peer(source)).wait_recv()

    for o, q in enumerate(zs):
        go(remote(small.at[own_block], small.at[own_block], zs_send.at[o], zs_recv.at[z],
                  z_peer(q)))
    for p in range(PIECES):
        for o, q in enumerate(zs):
            go(near_copy(o, q, z, p))
    for o, q in enumerate(zs):
        at = small.at[mine * nz + q]
        remote(at, at, zs_send.at[o], zs_recv.at[q], z_peer(q)).wait_recv()
    at = small_at(mine)
    for o, q in enumerate(dps):
        go(remote(at, at, ds_send.at[o], ds_recv.at[d], d_peer(q)))
    go(remote(at, at, cs_send.at[d], cs_recv.at[d], sibling))

    for p in range(PIECES):
        at = pl.ds(p * part, part)
        for o, q in enumerate(zs):
            near_copy(o, q, q, p).wait_recv()

        def lay_out(near32):
            for q in range(nz):
                near32[q * local_tokens:(q + 1) * local_tokens, :] = near[q, :, at].astype(
                    jnp.float32)
            hid[pl.ds(pl.multiple_of(mine * rows, rows), rows), at] = near32[...].astype(
                jnp.bfloat16)

        pl.run_scoped(lay_out, pltpu.VMEM((rows, part), jnp.float32))
        for o, q in enumerate(dps):
            to_dp(o, q, p)
        to_sibling(d, p)

    for o, q in enumerate(dps):
        at = small_at(q * 2 + k)
        remote(at, at, ds_send.at[o], ds_recv.at[q], d_peer(q)).wait_recv()
        go(remote(at, at, cs_send.at[q], cs_recv.at[q], sibling))

    groups = pl.cdiv(width, LANES)
    group_rows = 16 * pl.cdiv(groups, 16)
    offset = (d * nv + v) * width
    group_row = lax.broadcasted_iota(jnp.int32, (group_rows, kept), 0)
    lane_row = lax.broadcasted_iota(jnp.int32, (LANES, kept), 0)
    flat = group_row * LANES + lax.broadcasted_iota(jnp.int32, (group_rows, LANES), 1)
    per_step = 8 // local_tokens

    def scatter(step, carry):
        first = pl.multiple_of(step * 8, 8)
        found = []
        for i in range(8):
            block = step * per_step + i // local_tokens
            r = i % local_tokens
            ids = small[block, r:r + 1, :].astype(jnp.int32) - offset
            p = small[block, local_tokens + r:local_tokens + r + 1, :]
            target = small[block, 2 * local_tokens:, r:r + 1].astype(jnp.int32) - offset
            probs[pl.ds(first + i, 1), :] = p
            high = p.astype(jnp.bfloat16).astype(jnp.float32)
            inside = group_row == (ids >> 7)
            left = jnp.concatenate(
                [jnp.where(inside, high, 0.0), jnp.where(inside, p - high, 0.0)],
                axis=0).astype(jnp.bfloat16)
            right = jnp.where(lane_row == (ids & 127), 1.0, 0.0).astype(jnp.bfloat16)
            both = lax.dot_general(left, right, NT, preferred_element_type=jnp.float32)
            found.append(both[:group_rows] + both[group_rows:]
                         + jnp.where(flat == target, CE_WEIGHT, 0.0))
        cells[:, pl.ds(first, 8), :] = jnp.swapaxes(jnp.stack(found, axis=0), 0, 1)[:groups]
        return carry

    steps = tokens // 8 // PIECES
    for p in range(PIECES):
        for o, q in enumerate(dps):
            from_dp(q, p)
            to_sibling(q, p)
        if p == 0:
            for q in range(nd):
                at = small_at(q * 2 + 1 - k)
                remote(at, at, cs_send.at[q], cs_recv.at[q], sibling).wait_recv()
        lax.fori_loop(p * steps, (p + 1) * steps, scatter, 0)
    for p in range(PIECES):
        for q in range(nd):
            at = hid_at(q * 2 + 1 - k, p)
            remote(at, at, ch_send.at[p, q], ch_recv.at[p, q], sibling).wait_recv()
    for copy in sent:
        copy.wait_send()
    sent.clear()

    exp_part[...] = jnp.zeros_like(exp_part)
    dot_part[...] = jnp.zeros_like(dot_part)

    def finish_block(j, size, logits):
        for i in range(pl.cdiv(size, LANES)):
            n = min(LANES, size - i * LANES)
            group = j * (BLOCK // LANES) + i
            ratio = jnp.tanh(logits[:, i * LANES:i * LANES + n] * (1.0 / SOFT_CAP))
            capped = SOFT_CAP * ratio
            slope = 1.0 - ratio * ratio
            exps = jnp.exp(capped)
            sparse = cells[group, :, 0:n]
            cells[group, :, 0:n] = exps * slope
            grads[:, pl.ds(pl.multiple_of(group * LANES, LANES), n)] = (
                sparse * slope).astype(jnp.bfloat16)
            exp_part[:, 0:n] += exps
            dot_part[:, 0:n] += capped * sparse

    def raw_block(j, size):
        w = w_ref[pl.ds(pl.multiple_of(j * BLOCK, BLOCK), size), :]
        return lax.dot_general(w, hid[...], NT, preferred_element_type=jnp.float32)

    def all_blocks(raw):
        w_copy(0, BLOCK).wait()
        raw[0] = raw_block(0, BLOCK)

        def full_block(j, carry):
            w_copy(j, BLOCK).wait()
            finish_block(j - 1, BLOCK, raw[lax.rem(j + 1, 2)].T)
            raw[lax.rem(j, 2)] = raw_block(j, BLOCK)
            return carry

        lax.fori_loop(1, full_blocks, full_block, 0)
        previous = raw[(full_blocks - 1) % 2].T
        if tail:
            w_copy(full_blocks, tail).wait()
            logits = raw_block(full_blocks, tail).T
            finish_block(full_blocks - 1, BLOCK, previous)
            finish_block(full_blocks, tail, logits)
        else:
            finish_block(full_blocks - 1, BLOCK, previous)

    pl.run_scoped(all_blocks, pltpu.VMEM((2, BLOCK, tokens), jnp.float32))

    def cols(i):
        return pl.ds(starts[i], min(CHUNK, depth - starts[i]))

    def copy1(i, send):
        return remote(send.at[:, cols(i)], hid.at[pl.ds(0, half), cols(i)],
                      r1_send.at[i], r1_recv.at[i], sibling)

    def copy2(i, send, o, q, source):
        return remote(send.at[pl.ds(pl.multiple_of(q * rows, rows), rows), cols(i)],
                      hid.at[pl.ds(pl.multiple_of(half + source * rows, rows), rows), cols(i)],
                      r2_send.at[i, o], r2_recv.at[i, source], d_peer(q))

    def copy3(i, send3, o, q, source):
        return remote(send3.at[q, :, cols(i)], recv3.at[source, :, cols(i)],
                      r3_send.at[i, o], r3_recv.at[i, source], z_peer(q))

    def out_copy(start, size, sem):
        at = pl.ds(start, size)
        return pltpu.make_async_copy(out_ref.at[:, at], out_hbm.at[:, at], sem)

    def exp_product(i):
        total = None
        for first in range(0, groups, 8):
            last = min(groups, first + 8)
            rows_w = slice(first * LANES, min(width, last * LANES))
            left = jnp.concatenate([cells[g] for g in range(first, last)], axis=1)
            left = left[:, :rows_w.stop - rows_w.start].astype(jnp.bfloat16)
            term = jnp.dot(left, w_ref[rows_w, cols(i)], preferred_element_type=jnp.float32)
            total = term if total is None else total + term
        return total

    def grad_product(i):
        return jnp.dot(grads[...], w_ref[:, cols(i)], preferred_element_type=jnp.float32)

    def exchange_start(peers, me, slots, send, recv):
        slots[me] = totals[...]
        for o, peer in enumerate(peers):
            go(remote(slots.at[me], slots.at[me], send.at[o], recv.at[me], peer))

    def exchange_end(peers, slots, send, recv, axis):
        for o, peer in enumerate(peers):
            at = slots.at[peer[axis]]
            remote(at, at, send.at[o], recv.at[peer[axis]], peer).wait_recv()
        totals[...] = jnp.sum(slots[...], axis=0)

    def scale_group(group, n):
        at = pl.ds(pl.multiple_of(group * LANES, LANES), n)
        grads[:, at] = (column[:, 0:n] * cells[group, :, 0:n]
                        - LOSS_SCALE * grads[:, at].astype(jnp.float32)).astype(jnp.bfloat16)

    def scale_full(group, carry):
        scale_group(group, LANES)
        return carry

    def sum_chunks(own1, own2, send, send3):
        totals[...] = jnp.zeros_like(totals)
        totals[0:1, :] = jnp.sum(exp_part[...].T, axis=0, keepdims=True)
        totals[1:2, :] = jnp.sum(dot_part[...].T, axis=0, keepdims=True)
        exchange_start(peers_v, v, slots_v, tv_send, tv_recv)
        term = exp_product(0)
        own1[0] = term[:half]
        own1[1] = term[half:]
        exchange_end(peers_v, slots_v, tv_send, tv_recv, 1)
        exchange_start(peers_d, d, slots_d, td_send, td_recv)
        term = grad_product(0)
        exchange_end(peers_d, slots_d, td_send, td_recv, 0)

        spread = lambda row: jnp.broadcast_to(row, (LANES, tokens)).T
        exp_sum = spread(totals[0:1, :])
        exp_part[...] = exp_sum
        dot_part[...] = spread(totals[1:2, :])
        teacher_sum = jnp.sum(probs[...], axis=1, keepdims=True)
        scale = LOSS_SCALE * (teacher_sum + CE_WEIGHT) / exp_sum
        column[...] = scale

        def sum_cores(i, acc):
            size = acc.shape[1]
            acc = acc.reshape(nd, 2, rows, size)
            own1[i % 2, :, 0:size] = jnp.where(k == 0, acc[:, 0], acc[:, 1]).reshape(half, size)
            send[:, cols(i)] = jnp.where(k == 0, acc[:, 1], acc[:, 0]).reshape(half, size).astype(
                jnp.bfloat16)
            copy1(i, send).start()

        def sum_dp(i):
            size = cols(i).size
            copy1(i, send).wait()
            total = own1[i % 2, :, 0:size] + hid[0:half, cols(i)].astype(jnp.float32)
            send[:, cols(i)] = total.astype(jnp.bfloat16)
            for o, q in enumerate(dps):
                copy2(i, send, o, q, d).start()
            own1[i % 2, :, 0:size] = total
            own2[:, cols(i)] = own1[i % 2, pl.ds(pl.multiple_of(d * rows, rows), rows), 0:size]

        def sum_z(i):
            total = own2[:, cols(i)]
            for o, q in enumerate(dps):
                copy2(i, send, o, q, q).wait_recv()
                at = pl.ds(pl.multiple_of(half + q * rows, rows), rows)
                total = total + hid[at, cols(i)].astype(jnp.float32)
            for q in range(nz):
                send3[q, :, cols(i)] = total[q * local_tokens:(q + 1) * local_tokens]
            for o, q in enumerate(zs):
                copy3(i, send3, o, q, z).start()
            recv3[z, :, cols(i)] = send3[z, :, cols(i)]

        def put_out(i):
            for o, q in enumerate(zs):
                copy3(i, send3, o, q, q).wait_recv()
            total = recv3[0, :, cols(i)]
            for q in range(1, nz):
                total = total + recv3[q, :, cols(i)]
            out_ref[:, cols(i)] = total
            out_copy(starts[i], cols(i).size, out_sem.at[i]).start()

        size = cols(0).size
        first = jnp.concatenate([own1[0, :, 0:size], own1[1, :, 0:size]], axis=0)
        sum_cores(0, jnp.concatenate(
            [scale * first[:, at:at + LANES] - LOSS_SCALE * term[:, at:at + LANES]
             for at in range(0, size, LANES)], axis=1))
        lax.fori_loop(0, width // LANES, scale_full, 0)
        if width % LANES:
            scale_group(width // LANES, width % LANES)

        for i in range(chunks + 1 + 2 * LAG):
            if 0 < i < chunks:
                sum_cores(i, grad_product(i))
            if i == 1:
                own_row = mine * rows + z * local_tokens
                for r in range(local_tokens):
                    p = probs_in[r:r + 1, :]
                    out_ref[r:r + 1, depth:] = (
                        jnp.sum(p * jnp.log(p), axis=1, keepdims=True)
                        - dot_part[pl.ds(own_row + r, 1), :]
                        + (jnp.sum(p, axis=1, keepdims=True) + CE_WEIGHT)
                        * jnp.log(exp_part[pl.ds(own_row + r, 1), :]))
                out_copy(depth, LANES, out_sem.at[chunks]).start()
            if 0 <= i - 1 < chunks:
                sum_dp(i - 1)
            if 0 <= i - 1 - LAG < chunks:
                sum_z(i - 1 - LAG)
            if 0 <= i - 1 - 2 * LAG < chunks:
                put_out(i - 1 - 2 * LAG)

        for copy in sent:
            copy.wait_send()
        for i in range(chunks):
            for o, q in enumerate(dps):
                copy2(i, send, o, q, d).wait_send()
            for o, q in enumerate(zs):
                copy3(i, send3, o, q, z).wait_send()
            out_copy(starts[i], cols(i).size, out_sem.at[i]).wait()
        out_copy(depth, LANES, out_sem.at[chunks]).wait()

    pl.run_scoped(
        sum_chunks,
        pltpu.VMEM((2, half, CHUNK), jnp.float32),
        pltpu.VMEM((rows, depth), jnp.float32),
        pltpu.VMEM((half, depth), jnp.bfloat16),
        pltpu.VMEM((nz, local_tokens, depth), jnp.float32))


def per_device(nd, nv, hidden, head_weight, teacher_ids, teacher_probs, target_ids):
    local_tokens, depth = hidden.shape
    width = head_weight.shape[1]
    kept = teacher_ids.shape[1]
    count = nd * nv
    tokens = count * local_tokens
    nz = nv // 2
    rows = nz * local_tokens
    half = nd * rows
    chunks = pl.cdiv(depth, CHUNK)
    groups = pl.cdiv(width, LANES)
    f32, bf16 = jnp.float32, jnp.bfloat16
    sems = lambda *shape: pltpu.SemaphoreType.DMA(shape)
    hbm = pl.BlockSpec(memory_space=pl.ANY)
    out = pl.pallas_call(
        functools.partial(fused_kernel, nd, nv),
        in_specs=[hbm] * 5,
        out_specs=hbm,
        out_shape=jax.ShapeDtypeStruct((local_tokens, depth + LANES), f32),
        scratch_shapes=[
            pltpu.VMEM((local_tokens, kept), jnp.int32),
            pltpu.VMEM((local_tokens, kept), f32),
            pltpu.SMEM((local_tokens,), jnp.int32),
            pltpu.VMEM((local_tokens, depth + LANES), f32),
            sems(4),
            sems(chunks + 1),
            pltpu.VMEM((width, depth), bf16),
            pltpu.VMEM((tokens, depth), bf16),
            pltpu.VMEM((nz, local_tokens, depth), bf16),
            pltpu.VMEM((count, 2 * local_tokens + 1, kept), f32),
            pltpu.VMEM((groups, tokens, LANES), f32),
            pltpu.VMEM((tokens, width), bf16),
            pltpu.VMEM((tokens, kept), f32),
            pltpu.VMEM((tokens, LANES), f32),
            pltpu.VMEM((tokens, LANES), f32),
            pltpu.VMEM((tokens, LANES), f32),
            pltpu.VMEM((8, tokens), f32),
            pltpu.VMEM((nv, 8, tokens), f32),
            pltpu.VMEM((nd, 8, tokens), f32),
            pltpu.VMEM((nz, local_tokens, depth), f32),
            sems(pl.cdiv(width, BLOCK)),
            sems(nz), sems(nz), sems(PIECES, nz), sems(PIECES, nz),
            sems(nd), sems(nd), sems(PIECES, nd), sems(PIECES, nd),
            sems(nd), sems(nd), sems(PIECES, nd), sems(PIECES, nd),
            sems(nv), sems(nv), sems(nd), sems(nd),
            sems(chunks), sems(chunks),
            sems(chunks, nd), sems(chunks, nd),
            sems(chunks, nz), sems(chunks, nz),
        ],
        compiler_params=pltpu.CompilerParams(
            collective_id=0, has_side_effects=True, vmem_limit_bytes=64 * 1024 * 1024),
        cost_estimate=pl.CostEstimate(
            flops=4 * tokens * depth * width, bytes_accessed=2 * depth * width,
            transcendentals=2 * tokens * width),
        name="fused_head",
    )(hidden, teacher_ids, teacher_probs, target_ids, head_weight.T)
    return out[:, depth], out[:, :depth].astype(bf16)


def solution(mesh):
    in_specs = (
        P(AXES, None),
        P(None, AXES),
        P(AXES, None),
        P(AXES, None),
        P(AXES),
    )
    out_specs = (P(AXES), P(AXES, None))
    return jax.shard_map(
        functools.partial(per_device, mesh.shape["dp"], mesh.shape["vocab"]),
        mesh=mesh, in_specs=in_specs, out_specs=out_specs, check_vma=False
    )
```

```python
import functools
import jax
import jax.numpy as jnp
from jax import lax
from jax.experimental import pallas as pl
from jax.experimental.pallas import tpu as pltpu
from jax.sharding import PartitionSpec as P

SOFT_CAP = 30.0
CE_WEIGHT = 0.5
LOSS_SCALE = 8.0
BLOCK = 640
CHUNK = 768
LANES = 128
PIECES = 2
LAG = 2
AXES = ("dp", "vocab")
MESH = pl.DeviceIdType.MESH
NT = (((1,), (1,)), ((), ()))


def remote(src, dst, send, recv, peer):
    return pltpu.make_async_remote_copy(
        src_ref=src, dst_ref=dst, send_sem=send, recv_sem=recv,
        device_id=peer, device_id_type=MESH)


def fused_kernel(nd, nv, hid_hbm, ids_hbm, probs_hbm, targets_hbm, w_hbm, out_hbm,
                 ids_in, probs_in, targets_in, out_ref, in_sem, out_sem, w_ref, hid, small, cells, grads, probs, exp_part, dot_part,
                 slots, near,
                 direct_send, direct_recv, direct_sems,
                 w_sem, zs_send, zs_recv, zh_send, zh_recv, ds_send, ds_recv, dh_send, dh_recv,
                 cs_send, cs_recv, ch_send, ch_recv, t_send, t_recv,
                 r1_send, r1_recv, r2_send, r2_recv, r3_send, r3_recv):
    local_tokens, depth = hid_hbm.shape
    tokens = hid.shape[0]
    width = w_ref.shape[0]
    kept = ids_in.shape[1]
    nz = nv // 2
    rows = nz * local_tokens
    half = nd * rows
    starts = range(0, depth, CHUNK)
    chunks = len(starts)
    d, v = lax.axis_index("dp"), lax.axis_index("vocab")
    z, k = v // 2, lax.rem(v, 2)
    mine = d * 2 + k
    zs = [lax.rem(z + o, nz) for o in range(1, nz)]
    dps = [lax.rem(d + o, nd) for o in range(1, nd)]
    sibling = (d, z * 2 + 1 - k)
    z_peer = lambda q: (d, q * 2 + k)
    d_peer = lambda q: (q, v)

    full_blocks, tail = width // BLOCK, width % BLOCK
    pieces = full_blocks + (tail > 0)

    inputs = [
        pltpu.make_async_copy(src, dst, in_sem.at[i])
        for i, (src, dst) in enumerate((
            (ids_hbm, ids_in), (probs_hbm, probs_in), (targets_hbm, targets_in),
            (hid_hbm, near.at[z])))
    ]
    for copy in inputs:
        copy.start()

    barrier = pltpu.get_barrier_semaphore()
    peers = [(lax.rem(d + o // nv, nd), lax.rem(v + o % nv, nv)) for o in range(1, nd * nv)]
    for peer in peers:
        pl.semaphore_signal(barrier, inc=1, device_id=peer, device_id_type=MESH)

    def w_copy(j, size):
        at = pl.ds(pl.multiple_of(j * BLOCK, BLOCK), size)
        return pltpu.make_async_copy(w_hbm.at[at], w_ref.at[at], w_sem.at[j])

    def start_w(j, carry):
        w_copy(j, BLOCK).start()
        return carry

    lax.fori_loop(0, full_blocks, start_w, 0)
    if tail:
        w_copy(full_blocks, tail).start()

    for copy in inputs:
        copy.wait()
    own_block = mine * nz + z
    lane = lax.broadcasted_iota(jnp.int32, (1, kept), 1)
    target_row = jnp.zeros((1, kept), jnp.int32)
    for i in range(local_tokens):
        target_row = jnp.where(lane == i, targets_in[i], target_row)
    small[own_block, 0:local_tokens, :] = ids_in[...].astype(jnp.float32)
    small[own_block, local_tokens:2 * local_tokens, :] = probs_in[...]
    small[own_block, 2 * local_tokens:, :] = target_row.astype(jnp.float32)

    pl.semaphore_wait(barrier, nd * nv - 1)

    sent = []
    part = depth // PIECES

    def go(copy):
        copy.start()
        sent.append(copy)

    def small_at(group):
        return small.at[pl.ds(group * nz, nz)]

    def hid_at(group, p):
        return hid.at[pl.ds(pl.multiple_of(group * rows, rows), rows), pl.ds(p * part, part)]

    def near_copy(o, q, source, p):
        at = pl.ds(p * part, part)
        return remote(near.at[source, :, at], near.at[source, :, at],
                      zh_send.at[p, o], zh_recv.at[p, source], z_peer(q))

    def to_sibling(source, p):
        at = hid_at(source * 2 + k, p)
        go(remote(at, at, ch_send.at[p, source], ch_recv.at[p, source], sibling))

    def to_dp(o, q, p):
        at = hid_at(mine, p)
        go(remote(at, at, dh_send.at[p, o], dh_recv.at[p, d], d_peer(q)))

    def from_dp(source, p):
        at = hid_at(source * 2 + k, p)
        remote(at, at, dh_send.at[p, 0], dh_recv.at[p, source], d_peer(source)).wait_recv()

    for o, q in enumerate(zs):
        go(remote(small.at[own_block], small.at[own_block], zs_send.at[o], zs_recv.at[z],
                  z_peer(q)))
    for p in range(PIECES):
        for o, q in enumerate(zs):
            go(near_copy(o, q, z, p))
    for o, q in enumerate(zs):
        at = small.at[mine * nz + q]
        remote(at, at, zs_send.at[o], zs_recv.at[q], z_peer(q)).wait_recv()
    at = small_at(mine)
    for o, q in enumerate(dps):
        go(remote(at, at, ds_send.at[o], ds_recv.at[d], d_peer(q)))
    go(remote(at, at, cs_send.at[d], cs_recv.at[d], sibling))

    for p in range(PIECES):
        at = pl.ds(p * part, part)
        for o, q in enumerate(zs):
            near_copy(o, q, q, p).wait_recv()

        def lay_out(near32):
            for q in range(nz):
                near32[q * local_tokens:(q + 1) * local_tokens, :] = near[q, :, at].astype(
                    jnp.float32)
            hid[pl.ds(pl.multiple_of(mine * rows, rows), rows), at] = near32[...].astype(
                jnp.bfloat16)

        pl.run_scoped(lay_out, pltpu.VMEM((rows, part), jnp.float32))
        for o, q in enumerate(dps):
            to_dp(o, q, p)
        to_sibling(d, p)

    for o, q in enumerate(dps):
        at = small_at(q * 2 + k)
        remote(at, at, ds_send.at[o], ds_recv.at[q], d_peer(q)).wait_recv()
        go(remote(at, at, cs_send.at[q], cs_recv.at[q], sibling))

    groups = pl.cdiv(width, LANES)
    group_rows = 16 * pl.cdiv(groups, 16)
    offset = (d * nv + v) * width
    group_row = lax.broadcasted_iota(jnp.int32, (group_rows, kept), 0)
    lane_row = lax.broadcasted_iota(jnp.int32, (LANES, kept), 0)
    flat = group_row * LANES + lax.broadcasted_iota(jnp.int32, (group_rows, LANES), 1)
    per_step = 8 // local_tokens

    def scatter(step, carry):
        first = pl.multiple_of(step * 8, 8)
        found = []
        for i in range(8):
            block = step * per_step + i // local_tokens
            r = i % local_tokens
            ids = small[block, r:r + 1, :].astype(jnp.int32) - offset
            p = small[block, local_tokens + r:local_tokens + r + 1, :]
            target = small[block, 2 * local_tokens:, r:r + 1].astype(jnp.int32) - offset
            probs[pl.ds(first + i, 1), :] = p
            high = p.astype(jnp.bfloat16).astype(jnp.float32)
            inside = group_row == (ids >> 7)
            left = jnp.concatenate(
                [jnp.where(inside, high, 0.0), jnp.where(inside, p - high, 0.0)],
                axis=0).astype(jnp.bfloat16)
            right = jnp.where(lane_row == (ids & 127), 1.0, 0.0).astype(jnp.bfloat16)
            both = lax.dot_general(left, right, NT, preferred_element_type=jnp.float32)
            found.append(both[:group_rows] + both[group_rows:]
                         + jnp.where(flat == target, CE_WEIGHT, 0.0))
        cells[:, pl.ds(first, 8), :] = jnp.swapaxes(jnp.stack(found, axis=0), 0, 1)[:groups]
        return carry

    for q in range(nd):
        at = small_at(q * 2 + 1 - k)
        remote(at, at, cs_send.at[q], cs_recv.at[q], sibling).wait_recv()
    steps = tokens // 8
    marks = [0, steps * 3 // 8, steps * 7 // 8, steps]
    lax.fori_loop(marks[0], marks[1], scatter, 0, unroll=2)
    for p in range(PIECES):
        for o, q in enumerate(dps):
            from_dp(q, p)
            to_sibling(q, p)
        lax.fori_loop(marks[p + 1], marks[p + 2], scatter, 0, unroll=2)
    def from_sibling(p):
        for q in range(nd):
            at = hid_at(q * 2 + 1 - k, p)
            remote(at, at, ch_send.at[p, q], ch_recv.at[p, q], sibling).wait_recv()

    from_sibling(0)

    exp_part[...] = jnp.zeros_like(exp_part)
    dot_part[...] = jnp.zeros_like(dot_part)

    def finish_block(j, size, logits):
        for i in range(pl.cdiv(size, LANES)):
            n = min(LANES, size - i * LANES)
            group = j * (BLOCK // LANES) + i
            ratio = jnp.tanh(logits[:, i * LANES:i * LANES + n] * (1.0 / SOFT_CAP))
            capped = SOFT_CAP * ratio
            slope = 1.0 - ratio * ratio
            exps = jnp.exp(capped)
            sparse = cells[group, :, 0:n]
            cells[group, :, 0:n] = exps * slope
            grads[:, pl.ds(pl.multiple_of(group * LANES, LANES), n)] = (
                sparse * slope).astype(jnp.bfloat16)
            exp_part[:, 0:n] += exps
            dot_part[:, 0:n] += capped * sparse

    def raw_block(j, size):
        w = w_ref[pl.ds(pl.multiple_of(j * BLOCK, BLOCK), size), :]
        return lax.dot_general(w, hid[...], NT, preferred_element_type=jnp.float32)

    def piece_product(j, p):
        at = slice(p * part, (p + 1) * part)
        return lax.dot_general(w_ref[j * BLOCK:(j + 1) * BLOCK, at], hid[:, at], NT,
                               preferred_element_type=jnp.float32)

    def all_blocks(raw):
        for j in range(2):
            w_copy(j, BLOCK).wait()
            raw[j] = piece_product(j, 0)
        for p in range(1, PIECES):
            from_sibling(p)
        raw[0] += sum(piece_product(0, p) for p in range(1, PIECES))
        finish_block(0, BLOCK, raw[0].T)
        raw[1] += sum(piece_product(1, p) for p in range(1, PIECES))

        def full_block(j, carry):
            w_copy(j, BLOCK).wait()
            finish_block(j - 1, BLOCK, raw[lax.rem(j + 1, 2)].T)
            raw[lax.rem(j, 2)] = raw_block(j, BLOCK)
            return carry

        lax.fori_loop(2, full_blocks, full_block, 0)
        previous = raw[(full_blocks - 1) % 2].T
        if tail:
            w_copy(full_blocks, tail).wait()
            logits = raw_block(full_blocks, tail).T
            finish_block(full_blocks - 1, BLOCK, previous)
            finish_block(full_blocks, tail, logits)
        else:
            finish_block(full_blocks - 1, BLOCK, previous)

    pl.run_scoped(all_blocks, pltpu.VMEM((2, BLOCK, tokens), jnp.float32))
    for copy in sent:
        copy.wait_send()

    def cols(i):
        return pl.ds(starts[i], min(CHUNK, depth - starts[i]))

    def copy1(i, send):
        return remote(send.at[:, cols(i)], hid.at[pl.ds(0, half), cols(i)],
                      r1_send.at[i], r1_recv.at[i], sibling)

    def copy2(i, send, o, q, source):
        return remote(send.at[pl.ds(pl.multiple_of(q * rows, rows), rows), cols(i)],
                      hid.at[pl.ds(pl.multiple_of(half + source * rows, rows), rows), cols(i)],
                      r2_send.at[i, o], r2_recv.at[i, source], d_peer(q))

    def copy3(i, send3, o, q, source):
        return remote(send3.at[q, :, cols(i)], near.at[source, :, cols(i)],
                      r3_send.at[i, o], r3_recv.at[i, source], z_peer(q))

    def out_copy(start, size, sem):
        at = pl.ds(start, size)
        return pltpu.make_async_copy(out_ref.at[:, at], out_hbm.at[:, at], sem)

    def exp_product(i):
        total = None
        for first in range(0, groups, 8):
            last = min(groups, first + 8)
            rows_w = slice(first * LANES, min(width, last * LANES))
            left = jnp.concatenate([cells[g] for g in range(first, last)], axis=1)
            left = left[:, :rows_w.stop - rows_w.start].astype(jnp.bfloat16)
            term = jnp.dot(left, w_ref[rows_w, cols(i)], preferred_element_type=jnp.float32)
            total = term if total is None else total + term
        return total

    def grad_product(i):
        return jnp.dot(grads[...], w_ref[:, cols(i)], preferred_element_type=jnp.float32)

    twins = [(lax.rem(d + o // nz, nd), lax.rem(z + o % nz, nz)) for o in range(1, nd * nz)]

    def direct_copy(o, peer_d, peer_z, source):
        return remote(direct_send.at[peer_d * nz + peer_z], direct_recv.at[source],
                      direct_sems.at[0, o], direct_sems.at[1, source], (peer_d, peer_z * 2 + k))

    def total_copy(o, peer, source):
        at = slots.at[source]
        return remote(at, at, t_send.at[o], t_recv.at[source], peer)

    def scale_group(group, n):
        at = pl.ds(pl.multiple_of(group * LANES, LANES), n)
        grads[:, at] = (probs[:, 0:n] * cells[group, :, 0:n]
                        - LOSS_SCALE * grads[:, at].astype(jnp.float32)).astype(jnp.bfloat16)

    def scale_full(group, carry):
        scale_group(group, LANES)
        return carry

    def sum_chunks(own1, own2, send, send3):
        here = d * nv + v
        slots[here] = jnp.concatenate(
            [jnp.sum(exp_part[...].T, axis=0, keepdims=True),
             jnp.sum(dot_part[...].T, axis=0, keepdims=True)], axis=0)
        for o, peer in enumerate(peers):
            total_copy(o, peer, here).start()
        term = exp_product(0)
        own1[0] = term[:half]
        own1[1] = term[half:]
        term = grad_product(0)
        for o, (peer_d, peer_v) in enumerate(peers):
            total_copy(o, (peer_d, peer_v), peer_d * nv + peer_v).wait_recv()
        totals = jnp.sum(slots[...], axis=0)

        spread = lambda row: jnp.broadcast_to(row, (LANES, tokens)).T
        exp_sum = spread(totals[0:1, :])
        exp_part[...] = exp_sum
        dot_part[...] = spread(totals[1:2, :])
        teacher_sum = jnp.sum(probs[...], axis=1, keepdims=True)
        scale = LOSS_SCALE * (teacher_sum + CE_WEIGHT) / exp_sum
        probs[...] = scale

        def sum_cores(i, acc):
            size = acc.shape[1]
            acc = acc.reshape(nd, 2, rows, size)
            own1[i % 2, :, 0:size] = jnp.where(k == 0, acc[:, 0], acc[:, 1]).reshape(half, size)
            send[:, cols(i)] = jnp.where(k == 0, acc[:, 1], acc[:, 0]).reshape(half, size).astype(
                jnp.bfloat16)
            copy1(i, send).start()

        def sum_dp(i):
            size = cols(i).size
            copy1(i, send).wait()
            total = own1[i % 2, :, 0:size] + hid[0:half, cols(i)].astype(jnp.float32)
            send[:, cols(i)] = total.astype(jnp.bfloat16)
            for o, q in enumerate(dps):
                copy2(i, send, o, q, d).start()
            own1[i % 2, :, 0:size] = total
            own2[:, cols(i)] = own1[i % 2, pl.ds(pl.multiple_of(d * rows, rows), rows), 0:size]

        def sum_z(i):
            total = own2[:, cols(i)]
            for o, q in enumerate(dps):
                copy2(i, send, o, q, q).wait_recv()
                at = pl.ds(pl.multiple_of(half + q * rows, rows), rows)
                total = total + hid[at, cols(i)].astype(jnp.float32)
            for q in range(nz):
                send3[q, :, cols(i)] = total[q * local_tokens:(q + 1) * local_tokens].astype(
                    jnp.bfloat16)
            for o, q in enumerate(zs):
                copy3(i, send3, o, q, z).start()
            near[z, :, cols(i)] = send3[z, :, cols(i)]

        def put_out(i):
            for o, q in enumerate(zs):
                copy3(i, send3, o, q, q).wait_recv()
            out_ref[:, cols(i)] = jnp.sum(near[:, :, cols(i)].astype(jnp.float32), axis=0)
            out_copy(starts[i], cols(i).size, out_sem.at[i]).start()

        def send_last(i):
            size = cols(i).size
            copy1(i, send).wait()
            total = own1[i % 2, :, 0:size] + hid[0:half, cols(i)].astype(jnp.float32)
            for q in range(nd * nz):
                direct_send[q, :, 0:size] = total[q * local_tokens:(q + 1) * local_tokens].astype(
                    jnp.bfloat16)
            for o, (peer_d, peer_z) in enumerate(twins):
                direct_copy(o, peer_d, peer_z, d * nz + z).start()
            direct_recv[d * nz + z] = direct_send[d * nz + z]

        def put_last(i):
            size = cols(i).size
            for o, (peer_d, peer_z) in enumerate(twins):
                direct_copy(o, peer_d, peer_z, peer_d * nz + peer_z).wait_recv()
            out_ref[:, cols(i)] = jnp.sum(direct_recv[:, :, 0:size].astype(jnp.float32), axis=0)
            out_copy(starts[i], size, out_sem.at[i]).start()

        size = cols(0).size
        first = jnp.concatenate([own1[0, :, 0:size], own1[1, :, 0:size]], axis=0)
        sum_cores(0, jnp.concatenate(
            [scale * first[:, at:at + LANES] - LOSS_SCALE * term[:, at:at + LANES]
             for at in range(0, size, LANES)], axis=1))
        lax.fori_loop(0, width // LANES, scale_full, 0)
        if width % LANES:
            scale_group(width // LANES, width % LANES)

        for i in range(chunks + 2 * LAG):
            if 0 < i < chunks:
                sum_cores(i, grad_product(i))
            if i == 1:
                own_row = mine * rows + z * local_tokens
                for r in range(local_tokens):
                    p = probs_in[r:r + 1, :]
                    out_ref[r:r + 1, depth:] = (
                        jnp.sum(p * jnp.log(p), axis=1, keepdims=True)
                        - dot_part[pl.ds(own_row + r, 1), :]
                        + (jnp.sum(p, axis=1, keepdims=True) + CE_WEIGHT)
                        * jnp.log(exp_part[pl.ds(own_row + r, 1), :]))
                out_copy(depth, LANES, out_sem.at[chunks]).start()
            if i == chunks:
                send_last(i - 1)
            elif 0 < i < chunks:
                sum_dp(i - 1)
            if 0 <= i - 1 - LAG < chunks - 1:
                sum_z(i - 1 - LAG)
            if 0 <= i - 1 - 2 * LAG < chunks - 1:
                put_out(i - 1 - 2 * LAG)
        put_last(chunks - 1)

        for o, peer in enumerate(peers):
            total_copy(o, peer, here).wait_send()
        for i in range(chunks - 1):
            for o, q in enumerate(dps):
                copy2(i, send, o, q, d).wait_send()
            for o, q in enumerate(zs):
                copy3(i, send3, o, q, z).wait_send()
        for o, (peer_d, peer_z) in enumerate(twins):
            direct_copy(o, peer_d, peer_z, d * nz + z).wait_send()
        for i in range(chunks):
            out_copy(starts[i], cols(i).size, out_sem.at[i]).wait()
        out_copy(depth, LANES, out_sem.at[chunks]).wait()

    pl.run_scoped(
        sum_chunks,
        pltpu.VMEM((2, half, CHUNK), jnp.float32),
        pltpu.VMEM((rows, depth), jnp.float32),
        pltpu.VMEM((half, depth), jnp.bfloat16),
        pltpu.VMEM((nz, local_tokens, depth), jnp.bfloat16))


def per_device(nd, nv, hidden, head_weight, teacher_ids, teacher_probs, target_ids):
    local_tokens, depth = hidden.shape
    width = head_weight.shape[1]
    kept = teacher_ids.shape[1]
    count = nd * nv
    tokens = count * local_tokens
    nz = nv // 2
    rows = nz * local_tokens
    half = nd * rows
    chunks = pl.cdiv(depth, CHUNK)
    groups = pl.cdiv(width, LANES)
    f32, bf16 = jnp.float32, jnp.bfloat16
    sems = lambda *shape: pltpu.SemaphoreType.DMA(shape)
    hbm = pl.BlockSpec(memory_space=pl.ANY)
    out = pl.pallas_call(
        functools.partial(fused_kernel, nd, nv),
        in_specs=[hbm] * 5,
        out_specs=hbm,
        out_shape=jax.ShapeDtypeStruct((local_tokens, depth + LANES), f32),
        scratch_shapes=[
            pltpu.VMEM((local_tokens, kept), jnp.int32),
            pltpu.VMEM((local_tokens, kept), f32),
            pltpu.SMEM((local_tokens,), jnp.int32),
            pltpu.VMEM((local_tokens, depth + LANES), f32),
            sems(4),
            sems(chunks + 1),
            pltpu.VMEM((width, depth), bf16),
            pltpu.VMEM((tokens, depth), bf16),
            pltpu.VMEM((count, 2 * local_tokens + 1, kept), f32),
            pltpu.VMEM((groups, tokens, LANES), f32),
            pltpu.VMEM((tokens, width), bf16),
            pltpu.VMEM((tokens, LANES), f32),
            pltpu.VMEM((tokens, LANES), f32),
            pltpu.VMEM((tokens, LANES), f32),
            pltpu.VMEM((count, 2, tokens), f32),
            pltpu.VMEM((nz, local_tokens, depth), bf16),
            pltpu.VMEM((nd * nz, local_tokens, (depth - 1) % CHUNK + 1), bf16),
            pltpu.VMEM((nd * nz, local_tokens, (depth - 1) % CHUNK + 1), bf16),
            sems(2, nd * nz),
            sems(pl.cdiv(width, BLOCK)),
            sems(nz), sems(nz), sems(PIECES, nz), sems(PIECES, nz),
            sems(nd), sems(nd), sems(PIECES, nd), sems(PIECES, nd),
            sems(nd), sems(nd), sems(PIECES, nd), sems(PIECES, nd),
            sems(count), sems(count),
            sems(chunks), sems(chunks),
            sems(chunks, nd), sems(chunks, nd),
            sems(chunks, nz), sems(chunks, nz),
        ],
        compiler_params=pltpu.CompilerParams(
            collective_id=0, has_side_effects=True, vmem_limit_bytes=64 * 1024 * 1024),
        cost_estimate=pl.CostEstimate(
            flops=4 * tokens * depth * width, bytes_accessed=2 * depth * width,
            transcendentals=2 * tokens * width),
        name="fused_head",
    )(hidden, teacher_ids, teacher_probs, target_ids, head_weight.T)
    return out[:, depth], out[:, :depth].astype(bf16)


def solution(mesh):
    in_specs = (
        P(AXES, None),
        P(None, AXES),
        P(AXES, None),
        P(AXES, None),
        P(AXES),
    )
    out_specs = (P(AXES), P(AXES, None))
    return jax.shard_map(
        functools.partial(per_device, mesh.shape["dp"], mesh.shape["vocab"]),
        mesh=mesh, in_specs=in_specs, out_specs=out_specs, check_vma=False
    )
```

```python
import functools
import jax
import jax.numpy as jnp
from jax import lax
from jax.experimental import pallas as pl
from jax.experimental.pallas import tpu as pltpu
from jax.sharding import PartitionSpec as P

SOFT_CAP = 30.0
CE_WEIGHT = 0.5
LOSS_SCALE = 8.0
BLOCK = 640
CHUNK = 768
LANES = 128
PIECES = 2
LAG = 2
AXES = ("dp", "vocab")
MESH = pl.DeviceIdType.MESH
NT = (((1,), (1,)), ((), ()))


def remote(src, dst, send, recv, peer):
    return pltpu.make_async_remote_copy(
        src_ref=src, dst_ref=dst, send_sem=send, recv_sem=recv,
        device_id=peer, device_id_type=MESH)


def fused_kernel(nd, nv, hid_hbm, ids_hbm, probs_hbm, targets_hbm, w_hbm, out_hbm,
                 ids_in, probs_in, targets_in, out_ref, in_sem, out_sem, w_ref, hid, small, cells, grads, probs, exp_part, dot_part,
                 slots, near,
                 direct_send, direct_recv, direct_sems,
                 w_sem, zs_send, zs_recv, zh_send, zh_recv, ds_send, ds_recv, dh_send, dh_recv,
                 cs_send, cs_recv, ch_send, ch_recv, t_send, t_recv,
                 r1_send, r1_recv, r2_send, r2_recv, r3_send, r3_recv):
    local_tokens, depth = hid_hbm.shape
    tokens = hid.shape[0]
    width = w_ref.shape[0]
    kept = ids_in.shape[1]
    nz = nv // 2
    rows = nz * local_tokens
    half = nd * rows
    starts = range(0, depth, CHUNK)
    chunks = len(starts)
    d, v = lax.axis_index("dp"), lax.axis_index("vocab")
    z, k = v // 2, lax.rem(v, 2)
    mine = d * 2 + k
    zs = [lax.rem(z + o, nz) for o in range(1, nz)]
    dps = [lax.rem(d + o, nd) for o in range(1, nd)]
    sibling = (d, z * 2 + 1 - k)
    z_peer = lambda q: (d, q * 2 + k)
    d_peer = lambda q: (q, v)

    full_blocks, tail = width // BLOCK, width % BLOCK
    pieces = full_blocks + (tail > 0)

    inputs = [
        pltpu.make_async_copy(src, dst, in_sem.at[i])
        for i, (src, dst) in enumerate((
            (ids_hbm, ids_in), (probs_hbm, probs_in), (targets_hbm, targets_in),
            (hid_hbm, near.at[z])))
    ]
    for copy in inputs:
        copy.start()

    barrier = pltpu.get_barrier_semaphore()
    peers = [(lax.rem(d + o // nv, nd), lax.rem(v + o % nv, nv)) for o in range(1, nd * nv)]
    for peer in peers:
        pl.semaphore_signal(barrier, inc=1, device_id=peer, device_id_type=MESH)

    def w_copy(j, size):
        at = pl.ds(pl.multiple_of(j * BLOCK, BLOCK), size)
        return pltpu.make_async_copy(w_hbm.at[at], w_ref.at[at], w_sem.at[j])

    def start_w(j, carry):
        w_copy(j, BLOCK).start()
        return carry

    lax.fori_loop(0, full_blocks, start_w, 0)
    if tail:
        w_copy(full_blocks, tail).start()

    for copy in inputs:
        copy.wait()
    own_block = mine * nz + z
    lane = lax.broadcasted_iota(jnp.int32, (1, kept), 1)
    target_row = jnp.zeros((1, kept), jnp.int32)
    for i in range(local_tokens):
        target_row = jnp.where(lane == i, targets_in[i], target_row)
    small[own_block, 0:local_tokens, :] = ids_in[...].astype(jnp.float32)
    small[own_block, local_tokens:2 * local_tokens, :] = probs_in[...]
    small[own_block, 2 * local_tokens:, :] = target_row.astype(jnp.float32)

    pl.semaphore_wait(barrier, nd * nv - 1)

    sent = []
    part = depth // PIECES

    def go(copy):
        copy.start()
        sent.append(copy)

    def small_at(group):
        return small.at[pl.ds(group * nz, nz)]

    def hid_at(group, p):
        return hid.at[pl.ds(pl.multiple_of(group * rows, rows), rows), pl.ds(p * part, part)]

    def near_copy(o, q, source, p):
        at = pl.ds(p * part, part)
        return remote(near.at[source, :, at], near.at[source, :, at],
                      zh_send.at[p, o], zh_recv.at[p, source], z_peer(q))

    def to_sibling(source, p):
        at = hid_at(source * 2 + k, p)
        go(remote(at, at, ch_send.at[p, source], ch_recv.at[p, source], sibling))

    def to_dp(o, q, p):
        at = hid_at(mine, p)
        go(remote(at, at, dh_send.at[p, o], dh_recv.at[p, d], d_peer(q)))

    def from_dp(source, p):
        at = hid_at(source * 2 + k, p)
        remote(at, at, dh_send.at[p, 0], dh_recv.at[p, source], d_peer(source)).wait_recv()

    for o, q in enumerate(zs):
        go(remote(small.at[own_block], small.at[own_block], zs_send.at[o], zs_recv.at[z],
                  z_peer(q)))
    for p in range(PIECES):
        for o, q in enumerate(zs):
            go(near_copy(o, q, z, p))
    for o, q in enumerate(zs):
        at = small.at[mine * nz + q]
        remote(at, at, zs_send.at[o], zs_recv.at[q], z_peer(q)).wait_recv()
    at = small_at(mine)
    for o, q in enumerate(dps):
        go(remote(at, at, ds_send.at[o], ds_recv.at[d], d_peer(q)))
    go(remote(at, at, cs_send.at[d], cs_recv.at[d], sibling))

    for p in range(PIECES):
        at = pl.ds(p * part, part)
        for o, q in enumerate(zs):
            near_copy(o, q, q, p).wait_recv()

        def lay_out(near32):
            for q in range(nz):
                near32[q * local_tokens:(q + 1) * local_tokens, :] = near[q, :, at].astype(
                    jnp.float32)
            hid[pl.ds(pl.multiple_of(mine * rows, rows), rows), at] = near32[...].astype(
                jnp.bfloat16)

        pl.run_scoped(lay_out, pltpu.VMEM((rows, part), jnp.float32))
        for o, q in enumerate(dps):
            to_dp(o, q, p)
        to_sibling(d, p)

    for o, q in enumerate(dps):
        at = small_at(q * 2 + k)
        remote(at, at, ds_send.at[o], ds_recv.at[q], d_peer(q)).wait_recv()
        go(remote(at, at, cs_send.at[q], cs_recv.at[q], sibling))

    groups = pl.cdiv(width, LANES)
    group_rows = 16 * pl.cdiv(groups, 16)
    offset = (d * nv + v) * width
    group_row = lax.broadcasted_iota(jnp.int32, (group_rows, kept), 0)
    lane_row = lax.broadcasted_iota(jnp.int32, (LANES, kept), 0)
    flat = group_row * LANES + lax.broadcasted_iota(jnp.int32, (group_rows, LANES), 1)
    per_step = 8 // local_tokens

    def scatter(step, carry):
        first = pl.multiple_of(step * 8, 8)
        found = []
        for i in range(8):
            block = step * per_step + i // local_tokens
            r = i % local_tokens
            ids = small[block, r:r + 1, :].astype(jnp.int32) - offset
            p = small[block, local_tokens + r:local_tokens + r + 1, :]
            target = small[block, 2 * local_tokens:, r:r + 1].astype(jnp.int32) - offset
            probs[pl.ds(first + i, 1), :] = p
            high = p.astype(jnp.bfloat16).astype(jnp.float32)
            inside = group_row == (ids >> 7)
            left = jnp.concatenate(
                [jnp.where(inside, high, 0.0), jnp.where(inside, p - high, 0.0)],
                axis=0).astype(jnp.bfloat16)
            right = jnp.where(lane_row == (ids & 127), 1.0, 0.0).astype(jnp.bfloat16)
            both = lax.dot_general(left, right, NT, preferred_element_type=jnp.float32)
            found.append(both[:group_rows] + both[group_rows:]
                         + jnp.where(flat == target, CE_WEIGHT, 0.0))
        cells[:, pl.ds(first, 8), :] = jnp.swapaxes(jnp.stack(found, axis=0), 0, 1)[:groups]
        return carry

    for q in range(nd):
        at = small_at(q * 2 + 1 - k)
        remote(at, at, cs_send.at[q], cs_recv.at[q], sibling).wait_recv()
    steps = tokens // 8
    marks = [0, steps * 3 // 8, steps * 7 // 8, steps]
    lax.fori_loop(marks[0], marks[1], scatter, 0, unroll=2)
    for p in range(PIECES):
        for o, q in enumerate(dps):
            from_dp(q, p)
            to_sibling(q, p)
        lax.fori_loop(marks[p + 1], marks[p + 2], scatter, 0, unroll=2)
    def from_sibling(p):
        for q in range(nd):
            at = hid_at(q * 2 + 1 - k, p)
            remote(at, at, ch_send.at[p, q], ch_recv.at[p, q], sibling).wait_recv()

    from_sibling(0)

    exp_part[...] = jnp.zeros_like(exp_part)
    dot_part[...] = jnp.zeros_like(dot_part)

    def finish_block(j, size, logits):
        for i in range(pl.cdiv(size, LANES)):
            n = min(LANES, size - i * LANES)
            group = j * (BLOCK // LANES) + i
            ratio = jnp.tanh(logits[:, i * LANES:i * LANES + n] * (1.0 / SOFT_CAP))
            capped = SOFT_CAP * ratio
            slope = 1.0 - ratio * ratio
            exps = jnp.exp(capped)
            sparse = cells[group, :, 0:n]
            cells[group, :, 0:n] = exps * slope
            grads[:, pl.ds(pl.multiple_of(group * LANES, LANES), n)] = (
                sparse * slope).astype(jnp.bfloat16)
            exp_part[:, 0:n] += exps
            dot_part[:, 0:n] += capped * sparse

    def raw_block(j, size):
        w = w_ref[pl.ds(pl.multiple_of(j * BLOCK, BLOCK), size), :]
        return lax.dot_general(w, hid[...], NT, preferred_element_type=jnp.float32)

    def piece_product(j, p):
        at = slice(p * part, (p + 1) * part)
        return lax.dot_general(w_ref[j * BLOCK:(j + 1) * BLOCK, at], hid[:, at], NT,
                               preferred_element_type=jnp.float32)

    def all_blocks(raw):
        for j in range(2):
            w_copy(j, BLOCK).wait()
            raw[j] = piece_product(j, 0)
        for p in range(1, PIECES):
            from_sibling(p)
        raw[0] += sum(piece_product(0, p) for p in range(1, PIECES))
        finish_block(0, BLOCK, raw[0].T)
        raw[1] += sum(piece_product(1, p) for p in range(1, PIECES))

        def full_block(j, carry):
            w_copy(j, BLOCK).wait()
            finish_block(j - 1, BLOCK, raw[lax.rem(j + 1, 2)].T)
            raw[lax.rem(j, 2)] = raw_block(j, BLOCK)
            return carry

        lax.fori_loop(2, full_blocks, full_block, 0)
        previous = raw[(full_blocks - 1) % 2].T
        if tail:
            w_copy(full_blocks, tail).wait()
            logits = raw_block(full_blocks, tail).T
            finish_block(full_blocks - 1, BLOCK, previous)
            finish_block(full_blocks, tail, logits)
        else:
            finish_block(full_blocks - 1, BLOCK, previous)

    pl.run_scoped(all_blocks, pltpu.VMEM((2, BLOCK, tokens), jnp.float32))
    for copy in sent:
        copy.wait_send()

    def cols(i):
        return pl.ds(starts[i], min(CHUNK, depth - starts[i]))

    def copy1(i, send):
        return remote(send.at[:, cols(i)], hid.at[pl.ds(0, half), cols(i)],
                      r1_send.at[i], r1_recv.at[i], sibling)

    def copy2(i, send, o, q, source):
        return remote(send.at[pl.ds(pl.multiple_of(q * rows, rows), rows), cols(i)],
                      hid.at[pl.ds(pl.multiple_of(half + source * rows, rows), rows), cols(i)],
                      r2_send.at[i, o], r2_recv.at[i, source], d_peer(q))

    def copy3(i, send3, o, q, source):
        return remote(send3.at[q, :, cols(i)], near.at[source, :, cols(i)],
                      r3_send.at[i, o], r3_recv.at[i, source], z_peer(q))

    def out_copy(start, size, sem):
        at = pl.ds(start, size)
        return pltpu.make_async_copy(out_ref.at[:, at], out_hbm.at[:, at], sem)

    def exp_product(i):
        total = None
        for first in range(0, groups, 8):
            last = min(groups, first + 8)
            rows_w = slice(first * LANES, min(width, last * LANES))
            left = jnp.concatenate([cells[g] for g in range(first, last)], axis=1)
            left = left[:, :rows_w.stop - rows_w.start].astype(jnp.bfloat16)
            term = jnp.dot(left, w_ref[rows_w, cols(i)], preferred_element_type=jnp.float32)
            total = term if total is None else total + term
        return total

    def grad_product(i):
        return jnp.dot(grads[...], w_ref[:, cols(i)], preferred_element_type=jnp.float32)

    twins = [(lax.rem(d + o // nz, nd), lax.rem(z + o % nz, nz)) for o in range(1, nd * nz)]

    def direct_copy(o, peer_d, peer_z, source):
        return remote(direct_send.at[peer_d * nz + peer_z], direct_recv.at[source],
                      direct_sems.at[0, o], direct_sems.at[1, source], (peer_d, peer_z * 2 + k))

    def total_copy(o, peer, source):
        at = slots.at[source]
        return remote(at, at, t_send.at[o], t_recv.at[source], peer)

    def scale_group(group, n):
        at = pl.ds(pl.multiple_of(group * LANES, LANES), n)
        grads[:, at] = (probs[:, 0:n] * cells[group, :, 0:n]
                        - LOSS_SCALE * grads[:, at].astype(jnp.float32)).astype(jnp.bfloat16)

    def scale_full(group, carry):
        scale_group(group, LANES)
        return carry

    def sum_chunks(own1, own2, send, send3):
        here = d * nv + v
        slots[here] = jnp.concatenate(
            [jnp.sum(exp_part[...].T, axis=0, keepdims=True),
             jnp.sum(dot_part[...].T, axis=0, keepdims=True)], axis=0)
        for o, peer in enumerate(peers):
            total_copy(o, peer, here).start()
        term = exp_product(0)
        own1[0] = term[:half]
        own1[1] = term[half:]
        term = grad_product(0)
        for o, (peer_d, peer_v) in enumerate(peers):
            total_copy(o, (peer_d, peer_v), peer_d * nv + peer_v).wait_recv()
        totals = jnp.sum(slots[...], axis=0)

        spread = lambda row: jnp.broadcast_to(row, (LANES, tokens)).T
        exp_sum = spread(totals[0:1, :])
        exp_part[...] = exp_sum
        dot_part[...] = spread(totals[1:2, :])
        teacher_sum = jnp.sum(probs[...], axis=1, keepdims=True)
        scale = LOSS_SCALE * (teacher_sum + CE_WEIGHT) / exp_sum
        probs[...] = scale

        def sum_cores(i, acc):
            size = acc.shape[1]
            acc = acc.reshape(nd, 2, rows, size)
            own1[i % 2, :, 0:size] = jnp.where(k == 0, acc[:, 0], acc[:, 1]).reshape(half, size)
            send[:, cols(i)] = jnp.where(k == 0, acc[:, 1], acc[:, 0]).reshape(half, size).astype(
                jnp.bfloat16)
            copy1(i, send).start()

        def sum_dp(i):
            size = cols(i).size
            copy1(i, send).wait()
            total = own1[i % 2, :, 0:size] + hid[0:half, cols(i)].astype(jnp.float32)
            send[:, cols(i)] = total.astype(jnp.bfloat16)
            for o, q in enumerate(dps):
                copy2(i, send, o, q, d).start()
            own1[i % 2, :, 0:size] = total
            own2[:, cols(i)] = own1[i % 2, pl.ds(pl.multiple_of(d * rows, rows), rows), 0:size]

        def sum_z(i):
            total = own2[:, cols(i)]
            for o, q in enumerate(dps):
                copy2(i, send, o, q, q).wait_recv()
                at = pl.ds(pl.multiple_of(half + q * rows, rows), rows)
                total = total + hid[at, cols(i)].astype(jnp.float32)
            for q in range(nz):
                send3[q, :, cols(i)] = total[q * local_tokens:(q + 1) * local_tokens].astype(
                    jnp.bfloat16)
            for o, q in enumerate(zs):
                copy3(i, send3, o, q, z).start()
            near[z, :, cols(i)] = send3[z, :, cols(i)]

        def put_out(i):
            for o, q in enumerate(zs):
                copy3(i, send3, o, q, q).wait_recv()
            out_ref[:, cols(i)] = jnp.sum(near[:, :, cols(i)].astype(jnp.float32), axis=0)
            out_copy(starts[i], cols(i).size, out_sem.at[i]).start()

        def send_last(i):
            size = cols(i).size
            copy1(i, send).wait()
            total = own1[i % 2, :, 0:size] + hid[0:half, cols(i)].astype(jnp.float32)
            for q in range(nd * nz):
                direct_send[q, :, 0:size] = total[q * local_tokens:(q + 1) * local_tokens].astype(
                    jnp.bfloat16)
            for o, (peer_d, peer_z) in enumerate(twins):
                direct_copy(o, peer_d, peer_z, d * nz + z).start()
            direct_recv[d * nz + z] = direct_send[d * nz + z]

        def put_last(i):
            size = cols(i).size
            for o, (peer_d, peer_z) in enumerate(twins):
                direct_copy(o, peer_d, peer_z, peer_d * nz + peer_z).wait_recv()
            out_ref[:, cols(i)] = jnp.sum(direct_recv[:, :, 0:size].astype(jnp.float32), axis=0)
            out_copy(starts[i], size, out_sem.at[i]).start()

        size = cols(0).size
        first = jnp.concatenate([own1[0, :, 0:size], own1[1, :, 0:size]], axis=0)
        sum_cores(0, jnp.concatenate(
            [scale * first[:, at:at + LANES] - LOSS_SCALE * term[:, at:at + LANES]
             for at in range(0, size, LANES)], axis=1))
        lax.fori_loop(0, width // LANES, scale_full, 0)
        if width % LANES:
            scale_group(width // LANES, width % LANES)

        for i in range(chunks + 2 * LAG):
            if 0 < i < chunks:
                sum_cores(i, grad_product(i))
            if i == 1:
                own_row = mine * rows + z * local_tokens
                for r in range(local_tokens):
                    p = probs_in[r:r + 1, :]
                    out_ref[r:r + 1, depth:] = (
                        jnp.sum(p * jnp.log(p), axis=1, keepdims=True)
                        - dot_part[pl.ds(own_row + r, 1), :]
                        + (jnp.sum(p, axis=1, keepdims=True) + CE_WEIGHT)
                        * jnp.log(exp_part[pl.ds(own_row + r, 1), :]))
                out_copy(depth, LANES, out_sem.at[chunks]).start()
            if i == chunks:
                send_last(i - 1)
            elif 0 < i < chunks:
                sum_dp(i - 1)
            if 0 <= i - 1 - LAG < chunks - 1:
                sum_z(i - 1 - LAG)
            if 0 <= i - 1 - 2 * LAG < chunks - 1:
                put_out(i - 1 - 2 * LAG)
        put_last(chunks - 1)

        for o, peer in enumerate(peers):
            total_copy(o, peer, here).wait_send()
        for i in range(chunks - 1):
            for o, q in enumerate(dps):
                copy2(i, send, o, q, d).wait_send()
            for o, q in enumerate(zs):
                copy3(i, send3, o, q, z).wait_send()
        for o, (peer_d, peer_z) in enumerate(twins):
            direct_copy(o, peer_d, peer_z, d * nz + z).wait_send()
        for i in range(chunks):
            out_copy(starts[i], cols(i).size, out_sem.at[i]).wait()
        out_copy(depth, LANES, out_sem.at[chunks]).wait()

    pl.run_scoped(
        sum_chunks,
        pltpu.VMEM((2, half, CHUNK), jnp.float32),
        pltpu.VMEM((rows, depth), jnp.float32),
        pltpu.VMEM((half, depth), jnp.bfloat16),
        pltpu.VMEM((nz, local_tokens, depth), jnp.bfloat16))


def split_kernel(both_ref, loss_ref, grad_ref):
    local_tokens, depth = grad_ref.shape
    grad_ref[...] = both_ref[:, :depth].astype(jnp.bfloat16)
    for i in range(local_tokens):
        loss_ref[i] = jnp.max(both_ref[i:i + 1, depth:])


def per_device(nd, nv, hidden, head_weight, teacher_ids, teacher_probs, target_ids):
    local_tokens, depth = hidden.shape
    width = head_weight.shape[1]
    kept = teacher_ids.shape[1]
    count = nd * nv
    tokens = count * local_tokens
    nz = nv // 2
    rows = nz * local_tokens
    half = nd * rows
    chunks = pl.cdiv(depth, CHUNK)
    groups = pl.cdiv(width, LANES)
    f32, bf16 = jnp.float32, jnp.bfloat16
    sems = lambda *shape: pltpu.SemaphoreType.DMA(shape)
    hbm = pl.BlockSpec(memory_space=pl.ANY)
    out = pl.pallas_call(
        functools.partial(fused_kernel, nd, nv),
        in_specs=[hbm] * 5,
        out_specs=hbm,
        out_shape=jax.ShapeDtypeStruct((local_tokens, depth + LANES), f32),
        scratch_shapes=[
            pltpu.VMEM((local_tokens, kept), jnp.int32),
            pltpu.VMEM((local_tokens, kept), f32),
            pltpu.SMEM((local_tokens,), jnp.int32),
            pltpu.VMEM((local_tokens, depth + LANES), f32),
            sems(4),
            sems(chunks + 1),
            pltpu.VMEM((width, depth), bf16),
            pltpu.VMEM((tokens, depth), bf16),
            pltpu.VMEM((count, 2 * local_tokens + 1, kept), f32),
            pltpu.VMEM((groups, tokens, LANES), f32),
            pltpu.VMEM((tokens, width), bf16),
            pltpu.VMEM((tokens, LANES), f32),
            pltpu.VMEM((tokens, LANES), f32),
            pltpu.VMEM((tokens, LANES), f32),
            pltpu.VMEM((count, 2, tokens), f32),
            pltpu.VMEM((nz, local_tokens, depth), bf16),
            pltpu.VMEM((nd * nz, local_tokens, (depth - 1) % CHUNK + 1), bf16),
            pltpu.VMEM((nd * nz, local_tokens, (depth - 1) % CHUNK + 1), bf16),
            sems(2, nd * nz),
            sems(pl.cdiv(width, BLOCK)),
            sems(nz), sems(nz), sems(PIECES, nz), sems(PIECES, nz),
            sems(nd), sems(nd), sems(PIECES, nd), sems(PIECES, nd),
            sems(nd), sems(nd), sems(PIECES, nd), sems(PIECES, nd),
            sems(count), sems(count),
            sems(chunks), sems(chunks),
            sems(chunks, nd), sems(chunks, nd),
            sems(chunks, nz), sems(chunks, nz),
        ],
        compiler_params=pltpu.CompilerParams(
            collective_id=0, has_side_effects=True, vmem_limit_bytes=64 * 1024 * 1024),
        cost_estimate=pl.CostEstimate(
            flops=4 * tokens * depth * width, bytes_accessed=2 * depth * width,
            transcendentals=2 * tokens * width),
        name="fused_head",
    )(hidden, teacher_ids, teacher_probs, target_ids, head_weight.T)
    return tuple(pl.pallas_call(
        split_kernel,
        in_specs=[pl.BlockSpec(memory_space=pltpu.VMEM)],
        out_specs=[pl.BlockSpec(memory_space=pltpu.SMEM),
                   pl.BlockSpec(memory_space=pltpu.VMEM)],
        out_shape=[jax.ShapeDtypeStruct((local_tokens,), f32),
                   jax.ShapeDtypeStruct((local_tokens, depth), bf16)],
        name="split_outputs",
    )(out))


def solution(mesh):
    in_specs = (
        P(AXES, None),
        P(None, AXES),
        P(AXES, None),
        P(AXES, None),
        P(AXES),
    )
    out_specs = (P(AXES), P(AXES, None))
    return jax.shard_map(
        functools.partial(per_device, mesh.shape["dp"], mesh.shape["vocab"]),
        mesh=mesh, in_specs=in_specs, out_specs=out_specs, check_vma=False
    )
```

```python
import functools
import jax
import jax.numpy as jnp
from jax import lax
from jax.experimental import pallas as pl
from jax.experimental.pallas import tpu as pltpu
from jax.sharding import PartitionSpec as P

SOFT_CAP = 30.0
CE_WEIGHT = 0.5
LOSS_SCALE = 8.0
BLOCK = 640
CHUNK = 768
LANES = 128
PIECES = 2
LAG = 3
AXES = ("dp", "vocab")
MESH = pl.DeviceIdType.MESH
NT = (((1,), (1,)), ((), ()))


def remote(src, dst, send, recv, peer):
    return pltpu.make_async_remote_copy(
        src_ref=src, dst_ref=dst, send_sem=send, recv_sem=recv,
        device_id=peer, device_id_type=MESH)


def fused_kernel(nd, nv, hid_hbm, ids_hbm, probs_hbm, targets_hbm, w_hbm, out_hbm,
                 ids_in, probs_in, targets_in, out_ref, in_sem, out_sem, w_ref, hid, small, cells, grads, probs, exp_part, dot_part,
                 slots, near,
                 direct_send, direct_recv, direct_sems,
                 w_sem, zs_send, zs_recv, zh_send, zh_recv, ds_send, ds_recv, dh_send, dh_recv,
                 cs_send, cs_recv, ch_send, ch_recv, t_send, t_recv,
                 r1_send, r1_recv, r2_send, r2_recv, r3_send, r3_recv):
    local_tokens, depth = hid_hbm.shape
    tokens = hid.shape[0]
    width = w_ref.shape[0]
    kept = ids_in.shape[1]
    nz = nv // 2
    rows = nz * local_tokens
    half = nd * rows
    starts = range(0, depth, CHUNK)
    chunks = len(starts)
    d, v = lax.axis_index("dp"), lax.axis_index("vocab")
    z, k = v // 2, lax.rem(v, 2)
    mine = d * 2 + k
    zs = [lax.rem(z + o, nz) for o in range(1, nz)]
    dps = [lax.rem(d + o, nd) for o in range(1, nd)]
    sibling = (d, z * 2 + 1 - k)
    z_peer = lambda q: (d, q * 2 + k)
    d_peer = lambda q: (q, v)

    full_blocks, tail = width // BLOCK, width % BLOCK
    pieces = full_blocks + (tail > 0)

    inputs = [
        pltpu.make_async_copy(src, dst, in_sem.at[i])
        for i, (src, dst) in enumerate((
            (ids_hbm, ids_in), (probs_hbm, probs_in), (targets_hbm, targets_in),
            (hid_hbm, near.at[z])))
    ]
    for copy in inputs:
        copy.start()

    barrier = pltpu.get_barrier_semaphore()
    peers = [(lax.rem(d + o // nv, nd), lax.rem(v + o % nv, nv)) for o in range(1, nd * nv)]
    for peer in peers:
        pl.semaphore_signal(barrier, inc=1, device_id=peer, device_id_type=MESH)

    def w_copy(j, size):
        at = pl.ds(pl.multiple_of(j * BLOCK, BLOCK), size)
        return pltpu.make_async_copy(w_hbm.at[at], w_ref.at[at], w_sem.at[j])

    def start_w(j, carry):
        w_copy(j, BLOCK).start()
        return carry

    lax.fori_loop(0, full_blocks, start_w, 0)
    if tail:
        w_copy(full_blocks, tail).start()

    for copy in inputs:
        copy.wait()
    own_block = mine * nz + z
    lane = lax.broadcasted_iota(jnp.int32, (1, kept), 1)
    target_row = jnp.zeros((1, kept), jnp.int32)
    for i in range(local_tokens):
        target_row = jnp.where(lane == i, targets_in[i], target_row)
    small[own_block, 0:local_tokens, :] = ids_in[...].astype(jnp.float32)
    small[own_block, local_tokens:2 * local_tokens, :] = probs_in[...]
    small[own_block, 2 * local_tokens:, :] = target_row.astype(jnp.float32)

    pl.semaphore_wait(barrier, nd * nv - 1)

    sent = []
    part = depth // PIECES

    def go(copy):
        copy.start()
        sent.append(copy)

    def small_at(group):
        return small.at[pl.ds(group * nz, nz)]

    def hid_at(group, p):
        return hid.at[pl.ds(pl.multiple_of(group * rows, rows), rows), pl.ds(p * part, part)]

    def near_copy(o, q, source, p):
        at = pl.ds(p * part, part)
        return remote(near.at[source, :, at], near.at[source, :, at],
                      zh_send.at[p, o], zh_recv.at[p, source], z_peer(q))

    def to_sibling(source, p):
        at = hid_at(source * 2 + k, p)
        go(remote(at, at, ch_send.at[p, source], ch_recv.at[p, source], sibling))

    def to_dp(o, q, p):
        at = hid_at(mine, p)
        go(remote(at, at, dh_send.at[p, o], dh_recv.at[p, d], d_peer(q)))

    def from_dp(source, p):
        at = hid_at(source * 2 + k, p)
        remote(at, at, dh_send.at[p, 0], dh_recv.at[p, source], d_peer(source)).wait_recv()

    for o, q in enumerate(zs):
        go(remote(small.at[own_block], small.at[own_block], zs_send.at[o], zs_recv.at[z],
                  z_peer(q)))
    for p in range(PIECES):
        for o, q in enumerate(zs):
            go(near_copy(o, q, z, p))
    for o, q in enumerate(zs):
        at = small.at[mine * nz + q]
        remote(at, at, zs_send.at[o], zs_recv.at[q], z_peer(q)).wait_recv()
    at = small_at(mine)
    for o, q in enumerate(dps):
        go(remote(at, at, ds_send.at[o], ds_recv.at[d], d_peer(q)))
    go(remote(at, at, cs_send.at[d], cs_recv.at[d], sibling))

    for p in range(PIECES):
        at = pl.ds(p * part, part)
        for o, q in enumerate(zs):
            near_copy(o, q, q, p).wait_recv()

        def lay_out(near32):
            for q in range(nz):
                near32[q * local_tokens:(q + 1) * local_tokens, :] = near[q, :, at].astype(
                    jnp.float32)
            hid[pl.ds(pl.multiple_of(mine * rows, rows), rows), at] = near32[...].astype(
                jnp.bfloat16)

        pl.run_scoped(lay_out, pltpu.VMEM((rows, part), jnp.float32))
        for o, q in enumerate(dps):
            to_dp(o, q, p)
        to_sibling(d, p)

    for o, q in enumerate(dps):
        at = small_at(q * 2 + k)
        remote(at, at, ds_send.at[o], ds_recv.at[q], d_peer(q)).wait_recv()
        go(remote(at, at, cs_send.at[q], cs_recv.at[q], sibling))

    groups = pl.cdiv(width, LANES)
    group_rows = 16 * pl.cdiv(groups, 16)
    offset = (d * nv + v) * width
    group_row = lax.broadcasted_iota(jnp.int32, (group_rows, kept), 0)
    lane_row = lax.broadcasted_iota(jnp.int32, (LANES, kept), 0)
    flat = group_row * LANES + lax.broadcasted_iota(jnp.int32, (group_rows, LANES), 1)
    per_step = 8 // local_tokens

    def scatter(step, carry):
        first = pl.multiple_of(step * 8, 8)
        found = []
        for i in range(8):
            block = step * per_step + i // local_tokens
            r = i % local_tokens
            ids = small[block, r:r + 1, :].astype(jnp.int32) - offset
            p = small[block, local_tokens + r:local_tokens + r + 1, :]
            target = small[block, 2 * local_tokens:, r:r + 1].astype(jnp.int32) - offset
            probs[pl.ds(first + i, 1), :] = p
            high = p.astype(jnp.bfloat16).astype(jnp.float32)
            inside = group_row == (ids >> 7)
            left = jnp.concatenate(
                [jnp.where(inside, high, 0.0), jnp.where(inside, p - high, 0.0)],
                axis=0).astype(jnp.bfloat16)
            right = jnp.where(lane_row == (ids & 127), 1.0, 0.0).astype(jnp.bfloat16)
            both = lax.dot_general(left, right, NT, preferred_element_type=jnp.float32)
            found.append(both[:group_rows] + both[group_rows:]
                         + jnp.where(flat == target, CE_WEIGHT, 0.0))
        cells[:, pl.ds(first, 8), :] = jnp.swapaxes(jnp.stack(found, axis=0), 0, 1)[:groups]
        return carry

    for q in range(nd):
        at = small_at(q * 2 + 1 - k)
        remote(at, at, cs_send.at[q], cs_recv.at[q], sibling).wait_recv()
    steps = tokens // 8
    marks = [0, steps * 3 // 8, steps * 7 // 8, steps]
    lax.fori_loop(marks[0], marks[1], scatter, 0, unroll=2)
    for p in range(PIECES):
        for o, q in enumerate(dps):
            from_dp(q, p)
            to_sibling(q, p)
        lax.fori_loop(marks[p + 1], marks[p + 2], scatter, 0, unroll=2)
    def from_sibling(p):
        for q in range(nd):
            at = hid_at(q * 2 + 1 - k, p)
            remote(at, at, ch_send.at[p, q], ch_recv.at[p, q], sibling).wait_recv()

    from_sibling(0)

    exp_part[...] = jnp.zeros_like(exp_part)
    dot_part[...] = jnp.zeros_like(dot_part)

    def finish_block(j, size, logits):
        for i in range(pl.cdiv(size, LANES)):
            n = min(LANES, size - i * LANES)
            group = j * (BLOCK // LANES) + i
            ratio = jnp.tanh(logits[:, i * LANES:i * LANES + n] * (1.0 / SOFT_CAP))
            capped = SOFT_CAP * ratio
            slope = 1.0 - ratio * ratio
            exps = jnp.exp(capped)
            sparse = cells[group, :, 0:n]
            cells[group, :, 0:n] = exps * slope
            grads[:, pl.ds(pl.multiple_of(group * LANES, LANES), n)] = (
                sparse * slope).astype(jnp.bfloat16)
            exp_part[:, 0:n] += exps
            dot_part[:, 0:n] += capped * sparse

    def raw_block(j, size):
        w = w_ref[pl.ds(pl.multiple_of(j * BLOCK, BLOCK), size), :]
        return lax.dot_general(w, hid[...], NT, preferred_element_type=jnp.float32)

    def piece_product(j, p):
        at = slice(p * part, (p + 1) * part)
        return lax.dot_general(w_ref[j * BLOCK:(j + 1) * BLOCK, at], hid[:, at], NT,
                               preferred_element_type=jnp.float32)

    def all_blocks(raw):
        for j in range(2):
            w_copy(j, BLOCK).wait()
            raw[j] = piece_product(j, 0)
        for p in range(1, PIECES):
            from_sibling(p)
        raw[0] += sum(piece_product(0, p) for p in range(1, PIECES))
        finish_block(0, BLOCK, raw[0].T)
        raw[1] += sum(piece_product(1, p) for p in range(1, PIECES))

        def full_block(j, carry):
            w_copy(j, BLOCK).wait()
            finish_block(j - 1, BLOCK, raw[lax.rem(j + 1, 2)].T)
            raw[lax.rem(j, 2)] = raw_block(j, BLOCK)
            return carry

        lax.fori_loop(2, full_blocks, full_block, 0)
        previous = raw[(full_blocks - 1) % 2].T
        if tail:
            w_copy(full_blocks, tail).wait()
            logits = raw_block(full_blocks, tail).T
            finish_block(full_blocks - 1, BLOCK, previous)
            finish_block(full_blocks, tail, logits)
        else:
            finish_block(full_blocks - 1, BLOCK, previous)

    pl.run_scoped(all_blocks, pltpu.VMEM((2, BLOCK, tokens), jnp.float32))
    for copy in sent:
        copy.wait_send()

    def cols(i):
        return pl.ds(starts[i], min(CHUNK, depth - starts[i]))

    def copy1(i, send):
        return remote(send.at[:, cols(i)], hid.at[pl.ds(0, half), cols(i)],
                      r1_send.at[i], r1_recv.at[i], sibling)

    def copy2(i, send, o, q, source):
        return remote(send.at[pl.ds(pl.multiple_of(q * rows, rows), rows), cols(i)],
                      hid.at[pl.ds(pl.multiple_of(half + source * rows, rows), rows), cols(i)],
                      r2_send.at[i, o], r2_recv.at[i, source], d_peer(q))

    def copy3(i, send3, o, q, source):
        return remote(send3.at[q, :, cols(i)], near.at[source, :, cols(i)],
                      r3_send.at[i, o], r3_recv.at[i, source], z_peer(q))

    def out_copy(start, size, sem):
        at = pl.ds(start, size)
        return pltpu.make_async_copy(out_ref.at[:, at], out_hbm.at[:, at], sem)

    def exp_product(i):
        total = None
        for first in range(0, groups, 8):
            last = min(groups, first + 8)
            rows_w = slice(first * LANES, min(width, last * LANES))
            left = jnp.concatenate([cells[g] for g in range(first, last)], axis=1)
            left = left[:, :rows_w.stop - rows_w.start].astype(jnp.bfloat16)
            term = jnp.dot(left, w_ref[rows_w, cols(i)], preferred_element_type=jnp.float32)
            total = term if total is None else total + term
        return total

    def grad_product(i):
        return jnp.dot(grads[...], w_ref[:, cols(i)], preferred_element_type=jnp.float32)

    twins = [(lax.rem(d + o // nz, nd), lax.rem(z + o % nz, nz)) for o in range(1, nd * nz)]

    def direct_copy(o, peer_d, peer_z, source):
        return remote(direct_send.at[peer_d * nz + peer_z], direct_recv.at[source],
                      direct_sems.at[0, o], direct_sems.at[1, source], (peer_d, peer_z * 2 + k))

    def total_copy(o, peer, source):
        at = slots.at[source]
        return remote(at, at, t_send.at[o], t_recv.at[source], peer)

    def scale_group(group, n):
        at = pl.ds(pl.multiple_of(group * LANES, LANES), n)
        grads[:, at] = (probs[:, 0:n] * cells[group, :, 0:n]
                        - LOSS_SCALE * grads[:, at].astype(jnp.float32)).astype(jnp.bfloat16)

    def scale_full(group, carry):
        scale_group(group, LANES)
        return carry

    def sum_chunks(own1, own2, send, send3):
        here = d * nv + v
        slots[here] = jnp.concatenate(
            [jnp.sum(exp_part[...].T, axis=0, keepdims=True),
             jnp.sum(dot_part[...].T, axis=0, keepdims=True)], axis=0)
        for o, peer in enumerate(peers):
            total_copy(o, peer, here).start()
        term = exp_product(0)
        own1[0] = term[:half]
        own1[1] = term[half:]
        term = grad_product(0)
        for o, (peer_d, peer_v) in enumerate(peers):
            total_copy(o, (peer_d, peer_v), peer_d * nv + peer_v).wait_recv()
        totals = jnp.sum(slots[...], axis=0)

        spread = lambda row: jnp.broadcast_to(row, (LANES, tokens)).T
        exp_sum = spread(totals[0:1, :])
        exp_part[...] = exp_sum
        dot_part[...] = spread(totals[1:2, :])
        teacher_sum = jnp.sum(probs[...], axis=1, keepdims=True)
        scale = LOSS_SCALE * (teacher_sum + CE_WEIGHT) / exp_sum
        probs[...] = scale

        def sum_cores(i, acc):
            size = acc.shape[1]
            acc = acc.reshape(nd, 2, rows, size)
            own1[i % 2, :, 0:size] = jnp.where(k == 0, acc[:, 0], acc[:, 1]).reshape(half, size)
            send[:, cols(i)] = jnp.where(k == 0, acc[:, 1], acc[:, 0]).reshape(half, size).astype(
                jnp.bfloat16)
            copy1(i, send).start()

        def sum_dp(i):
            size = cols(i).size
            copy1(i, send).wait()
            total = own1[i % 2, :, 0:size] + hid[0:half, cols(i)].astype(jnp.float32)
            send[:, cols(i)] = total.astype(jnp.bfloat16)
            for o, q in enumerate(dps):
                copy2(i, send, o, q, d).start()
            own1[i % 2, :, 0:size] = total
            own2[:, cols(i)] = own1[i % 2, pl.ds(pl.multiple_of(d * rows, rows), rows), 0:size]

        def sum_z(i):
            total = own2[:, cols(i)]
            for o, q in enumerate(dps):
                copy2(i, send, o, q, q).wait_recv()
                at = pl.ds(pl.multiple_of(half + q * rows, rows), rows)
                total = total + hid[at, cols(i)].astype(jnp.float32)
            for q in range(nz):
                send3[q, :, cols(i)] = total[q * local_tokens:(q + 1) * local_tokens].astype(
                    jnp.bfloat16)
            for o, q in enumerate(zs):
                copy3(i, send3, o, q, z).start()
            near[z, :, cols(i)] = send3[z, :, cols(i)]

        def put_out(i):
            for o, q in enumerate(zs):
                copy3(i, send3, o, q, q).wait_recv()
            out_ref[:, cols(i)] = jnp.sum(near[:, :, cols(i)].astype(jnp.float32), axis=0)
            out_copy(starts[i], cols(i).size, out_sem.at[i]).start()

        def send_last(i):
            size = cols(i).size
            copy1(i, send).wait()
            total = own1[i % 2, :, 0:size] + hid[0:half, cols(i)].astype(jnp.float32)
            for q in range(nd * nz):
                direct_send[q, :, 0:size] = total[q * local_tokens:(q + 1) * local_tokens].astype(
                    jnp.bfloat16)
            for o, (peer_d, peer_z) in enumerate(twins):
                direct_copy(o, peer_d, peer_z, d * nz + z).start()
            direct_recv[d * nz + z] = direct_send[d * nz + z]

        def put_last(i):
            size = cols(i).size
            for o, (peer_d, peer_z) in enumerate(twins):
                direct_copy(o, peer_d, peer_z, peer_d * nz + peer_z).wait_recv()
            out_ref[:, cols(i)] = jnp.sum(direct_recv[:, :, 0:size].astype(jnp.float32), axis=0)
            out_copy(starts[i], size, out_sem.at[i]).start()

        size = cols(0).size
        first = jnp.concatenate([own1[0, :, 0:size], own1[1, :, 0:size]], axis=0)
        sum_cores(0, jnp.concatenate(
            [scale * first[:, at:at + LANES] - LOSS_SCALE * term[:, at:at + LANES]
             for at in range(0, size, LANES)], axis=1))
        lax.fori_loop(0, width // LANES, scale_full, 0)
        if width % LANES:
            scale_group(width // LANES, width % LANES)

        for i in range(chunks + 2 * LAG):
            if 0 < i < chunks:
                sum_cores(i, grad_product(i))
            if i == 1:
                own_row = mine * rows + z * local_tokens
                for r in range(local_tokens):
                    p = probs_in[r:r + 1, :]
                    out_ref[r:r + 1, depth:] = (
                        jnp.sum(p * jnp.log(p), axis=1, keepdims=True)
                        - dot_part[pl.ds(own_row + r, 1), :]
                        + (jnp.sum(p, axis=1, keepdims=True) + CE_WEIGHT)
                        * jnp.log(exp_part[pl.ds(own_row + r, 1), :]))
                out_copy(depth, LANES, out_sem.at[chunks]).start()
            if i == chunks:
                send_last(i - 1)
            elif 0 < i < chunks:
                sum_dp(i - 1)
            if 0 <= i - 1 - LAG < chunks - 1:
                sum_z(i - 1 - LAG)
            if 0 <= i - 1 - 2 * LAG < chunks - 1:
                put_out(i - 1 - 2 * LAG)
        put_last(chunks - 1)

        for o, peer in enumerate(peers):
            total_copy(o, peer, here).wait_send()
        for i in range(chunks - 1):
            for o, q in enumerate(dps):
                copy2(i, send, o, q, d).wait_send()
            for o, q in enumerate(zs):
                copy3(i, send3, o, q, z).wait_send()
        for o, (peer_d, peer_z) in enumerate(twins):
            direct_copy(o, peer_d, peer_z, d * nz + z).wait_send()
        for i in range(chunks):
            out_copy(starts[i], cols(i).size, out_sem.at[i]).wait()
        out_copy(depth, LANES, out_sem.at[chunks]).wait()

    pl.run_scoped(
        sum_chunks,
        pltpu.VMEM((2, half, CHUNK), jnp.float32),
        pltpu.VMEM((rows, depth), jnp.float32),
        pltpu.VMEM((half, depth), jnp.bfloat16),
        pltpu.VMEM((nz, local_tokens, depth), jnp.bfloat16))


def split_kernel(both_ref, loss_ref, grad_ref):
    local_tokens, depth = grad_ref.shape
    grad_ref[...] = both_ref[:, :depth].astype(jnp.bfloat16)
    for i in range(local_tokens):
        loss_ref[i] = jnp.max(both_ref[i:i + 1, depth:])


def per_device(nd, nv, hidden, head_weight, teacher_ids, teacher_probs, target_ids):
    local_tokens, depth = hidden.shape
    width = head_weight.shape[1]
    kept = teacher_ids.shape[1]
    count = nd * nv
    tokens = count * local_tokens
    nz = nv // 2
    rows = nz * local_tokens
    half = nd * rows
    chunks = pl.cdiv(depth, CHUNK)
    groups = pl.cdiv(width, LANES)
    f32, bf16 = jnp.float32, jnp.bfloat16
    sems = lambda *shape: pltpu.SemaphoreType.DMA(shape)
    hbm = pl.BlockSpec(memory_space=pl.ANY)
    out = pl.pallas_call(
        functools.partial(fused_kernel, nd, nv),
        in_specs=[hbm] * 5,
        out_specs=hbm,
        out_shape=jax.ShapeDtypeStruct((local_tokens, depth + LANES), f32),
        scratch_shapes=[
            pltpu.VMEM((local_tokens, kept), jnp.int32),
            pltpu.VMEM((local_tokens, kept), f32),
            pltpu.SMEM((local_tokens,), jnp.int32),
            pltpu.VMEM((local_tokens, depth + LANES), f32),
            sems(4),
            sems(chunks + 1),
            pltpu.VMEM((width, depth), bf16),
            pltpu.VMEM((tokens, depth), bf16),
            pltpu.VMEM((count, 2 * local_tokens + 1, kept), f32),
            pltpu.VMEM((groups, tokens, LANES), f32),
            pltpu.VMEM((tokens, width), bf16),
            pltpu.VMEM((tokens, LANES), f32),
            pltpu.VMEM((tokens, LANES), f32),
            pltpu.VMEM((tokens, LANES), f32),
            pltpu.VMEM((count, 2, tokens), f32),
            pltpu.VMEM((nz, local_tokens, depth), bf16),
            pltpu.VMEM((nd * nz, local_tokens, (depth - 1) % CHUNK + 1), bf16),
            pltpu.VMEM((nd * nz, local_tokens, (depth - 1) % CHUNK + 1), bf16),
            sems(2, nd * nz),
            sems(pl.cdiv(width, BLOCK)),
            sems(nz), sems(nz), sems(PIECES, nz), sems(PIECES, nz),
            sems(nd), sems(nd), sems(PIECES, nd), sems(PIECES, nd),
            sems(nd), sems(nd), sems(PIECES, nd), sems(PIECES, nd),
            sems(count), sems(count),
            sems(chunks), sems(chunks),
            sems(chunks, nd), sems(chunks, nd),
            sems(chunks, nz), sems(chunks, nz),
        ],
        compiler_params=pltpu.CompilerParams(
            collective_id=0, has_side_effects=True, vmem_limit_bytes=64 * 1024 * 1024),
        cost_estimate=pl.CostEstimate(
            flops=4 * tokens * depth * width, bytes_accessed=2 * depth * width,
            transcendentals=2 * tokens * width),
        name="fused_head",
    )(hidden, teacher_ids, teacher_probs, target_ids, head_weight.T)
    return tuple(pl.pallas_call(
        split_kernel,
        in_specs=[pl.BlockSpec(memory_space=pltpu.VMEM)],
        out_specs=[pl.BlockSpec(memory_space=pltpu.SMEM),
                   pl.BlockSpec(memory_space=pltpu.VMEM)],
        out_shape=[jax.ShapeDtypeStruct((local_tokens,), f32),
                   jax.ShapeDtypeStruct((local_tokens, depth), bf16)],
        name="split_outputs",
    )(out))


def solution(mesh):
    in_specs = (
        P(AXES, None),
        P(None, AXES),
        P(AXES, None),
        P(AXES, None),
        P(AXES),
    )
    out_specs = (P(AXES), P(AXES, None))
    return jax.shard_map(
        functools.partial(per_device, mesh.shape["dp"], mesh.shape["vocab"]),
        mesh=mesh, in_specs=in_specs, out_specs=out_specs, check_vma=False
    )
```
